32 devices in a mesh: frame: 4 (over x, core), clip: 8 (over z, y).
Axes of the slice: x: 2, y: 2, z: 4, core: 2. Of those that a mesh axis runs over, the one named last changes fastest.
Arguments:
- within_frame_asker_matrix: bfloat16 [8, 4, 128, 1536], P('clip', 'frame'), may hold values from -400 to 400
- within_frame_matcher_matrix: bfloat16 [8, 4, 128, 1536], P('clip', 'frame'), may hold values from -6 to 6
- within_frame_payload_matrix: bfloat16 [8, 4, 128, 1536], P('clip', 'frame'), may hold values from -5 to 5
- within_frame_upstream_derivative: bfloat16 [8, 4, 128, 1536], P('clip', 'frame'), may hold values from -48 to 48
- across_time_asker_matrix: bfloat16 [8, 4, 128, 1536], P('clip', 'frame'), may hold values from -400 to 400
- across_time_matcher_matrix: bfloat16 [8, 4, 128, 1536], P('clip', 'frame'), may hold values from -6 to 6
- across_time_payload_matrix: bfloat16 [8, 4, 128, 1536], P('clip', 'frame'), may hold values from -5 to 5
- across_time_upstream_derivative: bfloat16 [8, 4, 128, 1536], P('clip', 'frame'), may hold values from -48 to 48
- sharpness_factor: float32 [2, 12], replicated, may hold values from 0.7 to 1.4
Outputs:
- spatial_query_grad: bfloat16 [8, 4, 128, 1536], P('clip', 'frame')
- spatial_key_grad: bfloat16 [8, 4, 128, 1536], P('clip', 'frame')
- temporal_query_grad: bfloat16 [8, 4, 128, 1536], P('clip', 'frame')
- temporal_key_grad: bfloat16 [8, 4, 128, 1536], P('clip', 'frame')
- temporal_value_grad: bfloat16 [8, 4, 128, 1536], P('clip', 'frame')
- logit_scale_gradient: float32 [2, 12], replicated
The draws below stay inside these ranges and needn't reach their ends.
All inputs are finite; a program needn't handle non-finite values.
Results may differ from the reference program's by a relative error of at most 0.011.
Values may be sent and summed in bfloat16 or wider, within the bound.
A program may use at most 64 MiB of HBM per device.

```python
import math
import jax
import jax.numpy as jnp
from jax import lax

SHARD_CHANNELS = 12
K = 128
PATCHES = 128
FRAMES = 4
CLIPS = 8


def clipped_normal(key, full_shape):
    return jnp.clip(jax.random.normal(key, full_shape, jnp.float32), -5.0, 5.0)


def spatial_common(key):
    return clipped_normal(key, (CLIPS, FRAMES, PATCHES, SHARD_CHANNELS * K))


def temporal_common(key):
    return clipped_normal(jax.random.fold_in(key, 101), (CLIPS, FRAMES, PATCHES, SHARD_CHANNELS * K))


def rising_scale():
    clip_pos = jnp.arange(CLIPS, dtype=jnp.float32) / max(CLIPS - 1, 1)
    frame_pos = jnp.arange(FRAMES, dtype=jnp.float32) / max(FRAMES - 1, 1)
    return jnp.exp(math.log(3.0) * (clip_pos[:, None] + frame_pos[None, :]))[:, :, None, None]


def draw_within_frame_asker_matrix(key, part):
    key = jax.random.fold_in(key, 5)
    full_shape = (CLIPS, FRAMES, PATCHES, SHARD_CHANNELS * K)
    return clipped_normal(key, full_shape).astype(jnp.bfloat16)


def draw_within_frame_matcher_matrix(key, part):
    common = spatial_common(key)
    return common.astype(jnp.bfloat16)


def draw_across_time_asker_matrix(key, part):
    key = jax.random.fold_in(key, 13)
    full_shape = (CLIPS, FRAMES, PATCHES, SHARD_CHANNELS * K)
    return clipped_normal(key, full_shape).astype(jnp.bfloat16)


def draw_across_time_matcher_matrix(key, part):
    common = temporal_common(key)
    return common.astype(jnp.bfloat16)


def draw_within_frame_upstream_derivative(key, part):
    key = jax.random.fold_in(key, 7)
    full_shape = (CLIPS, FRAMES, PATCHES, SHARD_CHANNELS * K)
    return (clipped_normal(key, full_shape) * rising_scale()).astype(jnp.bfloat16)


def draw_across_time_upstream_derivative(key, part):
    key = jax.random.fold_in(key, 9)
    full_shape = (CLIPS, FRAMES, PATCHES, SHARD_CHANNELS * K)
    return (clipped_normal(key, full_shape) * rising_scale()).astype(jnp.bfloat16)


def levels(stream_key, extent, pieces, low, top_value):
    def one(axis_at, shards_of):
        steps = jax.random.uniform(jax.random.fold_in(jax.random.fold_in(stream_key, 6), axis_at), (shards_of,), jnp.float32, low / len(pieces), top_value / len(pieces))
        return jnp.repeat(jnp.exp(steps), extent[axis_at] // shards_of).reshape((-1,) + (1,) * (len(extent) - axis_at - 1))

    loudness = one(*pieces[0])
    for cut in pieces[1:]:
        loudness = loudness * one(*cut)
    return loudness


def normal_values(key, shape, scale, bound, cuts=(), kind=jnp.bfloat16):
    gain = levels(key, shape, cuts, -0.22, 0.18) if cuts else 1.0
    values = jax.random.normal(key, shape, jnp.float32) * scale * gain
    return jnp.minimum(jnp.maximum(values, -bound), bound).astype(kind)


def setup_inputs(seed: int = 0) -> dict:
    key_of = jax.random.split(jax.random.key(seed), 10)
    return {
        "within_frame_asker_matrix": draw_within_frame_asker_matrix(jax.random.fold_in(key_of[9], 71), 0),
        "within_frame_matcher_matrix": draw_within_frame_matcher_matrix(jax.random.fold_in(key_of[9], 71), 0),
        "within_frame_payload_matrix": normal_values(key_of[2], (CLIPS, FRAMES, PATCHES, SHARD_CHANNELS * K), 1.0, 5.0, ((0, 8), (1, 4))),
        "within_frame_upstream_derivative": draw_within_frame_upstream_derivative(jax.random.fold_in(key_of[9], 71), 0),
        "across_time_asker_matrix": draw_across_time_asker_matrix(jax.random.fold_in(key_of[9], 71), 0),
        "across_time_matcher_matrix": draw_across_time_matcher_matrix(jax.random.fold_in(key_of[9], 71), 0),
        "across_time_payload_matrix": normal_values(key_of[6], (CLIPS, FRAMES, PATCHES, SHARD_CHANNELS * K), 1.0, 5.0, ((0, 8), (1, 4))),
        "across_time_upstream_derivative": draw_across_time_upstream_derivative(jax.random.fold_in(key_of[9], 71), 0),
        "sharpness_factor": jnp.clip(jnp.exp(jax.random.uniform(key_of[8], (2, SHARD_CHANNELS), jnp.float32, math.log(0.7), math.log(1.4))), 0.7, 1.4),
    }


def softmax_mixing_reverse_pass(queries, key_rows, values, cotangent, temper_row, causal):
    head_width = queries.shape[-1]
    queries_f = queries.astype(jnp.float32)
    keys_f = key_rows.astype(jnp.float32)
    values_f = values.astype(jnp.float32)
    cotangent_f = cotangent.astype(jnp.float32)
    raw_scores = jnp.einsum('lbhk,mbhk->bhlm', queries_f, keys_f) / math.sqrt(head_width)
    scores = temper_row[None, :, None, None] * raw_scores
    if causal:
        length = queries.shape[0]
        row_index = lax.broadcasted_iota(jnp.int32, (length, length), 0)
        col_index = lax.broadcasted_iota(jnp.int32, (length, length), 1)
        scores = jnp.where(col_index <= row_index, scores, -jnp.inf)
    row_max = lax.optimization_barrier(jnp.max(scores, axis=-1, keepdims=True))
    exponent = jnp.exp(scores - row_max)
    soft_weights = exponent / lax.optimization_barrier(jnp.sum(exponent, axis=-1, keepdims=True))
    weights_low = lax.optimization_barrier(soft_weights.astype(jnp.bfloat16)).astype(jnp.float32)
    value_grad = jnp.einsum('bhlm,lbhk->mbhk', weights_low, cotangent_f)
    weight_grad = jnp.einsum('lbhk,mbhk->bhlm', cotangent_f, values_f)
    row_delta = lax.optimization_barrier(jnp.sum(soft_weights * weight_grad, axis=-1, keepdims=True))
    score_grad = soft_weights * (weight_grad - row_delta)
    score_low = lax.optimization_barrier(score_grad.astype(jnp.bfloat16)).astype(jnp.float32)
    factor = (temper_row / math.sqrt(head_width))[None, None, :, None]
    query_grad = jnp.einsum('bhlm,mbhk->lbhk', score_low, keys_f) * factor
    key_grad = jnp.einsum('bhlm,lbhk->mbhk', score_low, queries_f) * factor
    payload_derivative_share = lax.optimization_barrier(jnp.sum(score_grad * raw_scores, axis=(2, 3)))
    return (query_grad.astype(jnp.bfloat16), key_grad.astype(jnp.bfloat16), value_grad.astype(jnp.bfloat16), payload_derivative_share)

def reference(within_frame_asker_matrix, within_frame_matcher_matrix, within_frame_payload_matrix, within_frame_upstream_derivative, across_time_asker_matrix, across_time_matcher_matrix, across_time_payload_matrix, across_time_upstream_derivative, sharpness_factor):
    clips, frames, patches, features = within_frame_asker_matrix.shape
    channel_bundle = sharpness_factor.shape[1]
    head_width = features // channel_bundle

    def spatial_block(layer_sequence):
        return softmax_mixing_reverse_pass(layer_sequence[0], layer_sequence[1], layer_sequence[2], layer_sequence[3], sharpness_factor[0], False)

    def temporal_block(layer_sequence):
        return softmax_mixing_reverse_pass(layer_sequence[0], layer_sequence[1], layer_sequence[2], layer_sequence[3], sharpness_factor[1], True)
    spatial_in = tuple((block.reshape(clips * frames, patches, 1, channel_bundle, head_width) for block in (within_frame_asker_matrix, within_frame_matcher_matrix, within_frame_payload_matrix, within_frame_upstream_derivative)))
    spatial_result = lax.map(spatial_block, spatial_in)
    temporal_in = tuple((block.reshape(clips, frames, patches, channel_bundle, head_width) for block in (across_time_asker_matrix, across_time_matcher_matrix, across_time_payload_matrix, across_time_upstream_derivative)))
    temporal_result = lax.map(temporal_block, temporal_in)
    scale_norm = 1.0 / math.sqrt(clips * frames * patches)
    logit_scale_gradient = jnp.stack([lax.optimization_barrier(jnp.sum(spatial_result[3], axis=(0, 1))), lax.optimization_barrier(jnp.sum(temporal_result[3], axis=(0, 1)))]) * scale_norm
    entire_result = (clips, frames, patches, features)
    return (spatial_result[0].reshape(entire_result), spatial_result[1].reshape(entire_result), temporal_result[0].reshape(entire_result), temporal_result[1].reshape(entire_result), temporal_result[2].reshape(entire_result), logit_scale_gradient)
```

```python
import functools
import math

import jax
import jax.numpy as jnp
from jax import lax
from jax.experimental import pallas as pl
from jax.experimental.pallas import tpu as pltpu
from jax.sharding import PartitionSpec as P

F32 = jnp.float32
BF16 = jnp.bfloat16
LANES = 128
HALF = 64
CHUNKS = 4
HEADS_AT_ONCE = 4


def contract(left, right, left_dim, right_dim):
    return lax.dot_general(
        left, right, (((left_dim,), (right_dim,)), ((), ())), preferred_element_type=F32
    )


def kernel(
    frames,
    clips,
    heads,
    scale_norm,
    sharp,
    sq_in,
    sk_in,
    sv_in,
    sc_in,
    tq_in,
    tk_in,
    tv_in,
    tc_in,
    sdq,
    sdk,
    tdq,
    tdk,
    tdv,
    logit,
    sq,
    sk,
    sv,
    sc,
    tq,
    tk,
    tv,
    tc,
    far,
    raw_s,
    grad_s,
    mix_out,
    mix_in,
    logit_rows,
    logit_heads,
    sum_frame,
    sum_clip,
    load_sem,
    cross_send,
    mate_send,
    pass_send,
    mix_send,
    frame_send,
    clip_send,
    far_recv,
    mix_recv,
    frame_recv,
    clip_recv,
):
    me = lax.axis_index("frame")
    clip = lax.axis_index("clip")
    chips = frames // 2
    chip, core = me // 2, lax.rem(me, 2)
    mate = chip * 2 + 1 - core
    patches, features = sq.shape
    width = features // heads
    block = patches // CHUNKS
    inv = 1.0 / math.sqrt(width)
    others = range(1, chips)

    def rows(c):
        return pl.ds(pl.multiple_of(c * block, block), block)

    def cols(h):
        return slice(h * width, (h + 1) * width)

    def remote(src, dst, send, recv, axis, target):
        return pltpu.make_async_remote_copy(
            src_ref=src,
            dst_ref=dst,
            send_sem=send,
            recv_sem=recv,
            device_id={axis: target},
            device_id_type=pl.DeviceIdType.MESH,
        )

    def far_copy(part, slot, c, src, send, target):
        return remote(
            src.at[rows(c)], far.at[part, slot, rows(c)], send, far_recv.at[part, slot, c], "frame", target
        )

    def far_here(part, slot, c):
        remote(
            far.at[part, slot, rows(c)],
            far.at[part, slot, rows(c)],
            mate_send.at[part, c],
            far_recv.at[part, slot, c],
            "frame",
            mate,
        ).wait_recv()

    def chip_at(d):
        return lax.rem(chip + d, chips)

    loads = [
        pltpu.make_async_copy(src, dst, load_sem.at[i])
        for i, (src, dst) in enumerate(
            ((sq_in, sq), (sk_in, sk), (sv_in, sv), (sc_in, sc), (tq_in, tq), (tk_in, tk), (tv_in, tv), (tc_in, tc))
        )
    ]
    for load in loads:
        load.start()

    barrier = pltpu.get_barrier_semaphore()
    for d in range(1, frames):
        pl.semaphore_signal(
            barrier, inc=1, device_id={"frame": lax.rem(me + d, frames)}, device_id_type=pl.DeviceIdType.MESH
        )
    for d in range(1, clips):
        pl.semaphore_signal(
            barrier, inc=1, device_id={"clip": lax.rem(clip + d, clips)}, device_id_type=pl.DeviceIdType.MESH
        )
    pl.semaphore_wait(barrier, frames + clips - 2)

    def send_to(target, c, sems):
        @pl.when(target < me)
        def _():
            far_copy(0, me, c, tq_in, sems(0), target).start()
            far_copy(1, me, c, tc_in, sems(1), target).start()

        @pl.when(target > me)
        def _():
            far_copy(0, me, c, tk_in, sems(0), target).start()
            far_copy(1, me, c, tv_in, sems(1), target).start()

    for c in range(CHUNKS):
        for d in others:
            send_to(chip_at(d) * 2 + core, c, lambda part: cross_send.at[part, d, c])
        send_to(mate, c, lambda part: mate_send.at[part, c])

    logit_rows[...] = jnp.zeros_like(logit_rows)
    logit_heads[...] = jnp.zeros_like(logit_heads)
    lane_row = lax.broadcasted_iota(jnp.int32, (1, LANES), 1)
    sharp_lanes = jnp.zeros((1, LANES), F32)
    for h in range(heads):
        sharp_lanes = jnp.where(lane_row == h, sharp[1, h], sharp_lanes)
    lane = lax.broadcasted_iota(jnp.int32, (block, LANES), 1)

    for load in loads:
        load.wait()

    def spatial(h):
        at = pl.ds(pl.multiple_of(h * width, width), width)
        query, key, value, cotangent = sq[:, at], sk[:, at], sv[:, at], sc[:, at]
        sharpness = sharp[0, h]
        raw = contract(query, key, 1, 1) * inv
        scores = raw * sharpness
        exponent = jnp.exp(scores - jnp.max(scores, axis=1, keepdims=True))
        weights = exponent * (1.0 / jnp.sum(exponent, axis=1, keepdims=True))
        weight_grad = contract(cotangent, value, 1, 1)
        delta = jnp.sum(weights * weight_grad, axis=1, keepdims=True)
        score_grad = weights * (weight_grad - delta)
        low = score_grad.astype(BF16)
        factor = sharpness * inv
        sdq[:, at] = (contract(low, key, 1, 0) * factor).astype(BF16)
        sdk[:, at] = (contract(low, query, 0, 0) * factor).astype(BF16)
        logit_heads[pl.ds(h, 1), :] = jnp.sum(score_grad * raw, axis=0, keepdims=True)

    def dots(left, right):
        out = jnp.zeros((block, LANES), F32)
        for h in range(heads):
            product = left(cols(h)).astype(F32) * right(cols(h)).astype(F32)
            out = jnp.where(lane == h, jnp.sum(product, axis=1, keepdims=True), out)
        return out

    def spread(mix, at):
        return jnp.broadcast_to(mix[:, at : at + 1], (block, width))

    def row_part(c):
        r = rows(c)
        for part in range(2):
            far_here(part, mate, c)
            for d in others:
                far_here(part, chip_at(d) * 2 + 1 - core, c)
        raw_own = dots(lambda s: tq[r, s], lambda s: tk[r, s]) * inv
        grad_own = dots(lambda s: tc[r, s], lambda s: tv[r, s])

        @pl.loop(0, me)
        def _(j):
            raw_s[j] = dots(lambda s: tq[r, s], lambda s: far[0, j, r, s]) * inv
            grad_s[j] = dots(lambda s: tc[r, s], lambda s: far[1, j, r, s])

        top = lax.fori_loop(
            0, me, lambda j, top: jnp.maximum(top, raw_s[j] * sharp_lanes), raw_own * sharp_lanes
        )

        def add(j, carry):
            exponent = jnp.exp(raw_s[j] * sharp_lanes - top)
            return carry[0] + exponent, carry[1] + exponent * grad_s[j]

        exponent_own = jnp.exp(raw_own * sharp_lanes - top)
        total, mean = lax.fori_loop(0, me, add, (exponent_own, exponent_own * grad_own))
        over = 1.0 / total
        delta = mean * over

        def mixed(exponent, raw, grad):
            weights = exponent * over
            score_grad = weights * (grad - delta)
            logit_rows[...] += score_grad * raw
            return jnp.where(lane < HALF, weights, pltpu.roll(score_grad, HALF, 1)).astype(BF16)

        mix_out[me, r] = mixed(exponent_own, raw_own, grad_own)

        @pl.loop(0, me)
        def _(j):
            mix_out[j, r] = mixed(jnp.exp(raw_s[j] * sharp_lanes - top), raw_s[j], grad_s[j])
            remote(
                mix_out.at[j, r], mix_in.at[me, r], mix_send.at[j, c], mix_recv.at[me, c], "frame", j
            ).start()

        for first in range(0, heads, HEADS_AT_ONCE):
            some = range(first, min(first + HEADS_AT_ONCE, heads))

            def add_key(j, sums):
                mix = mix_out[j, r].astype(F32)
                return tuple(
                    t + spread(mix, HALF + h) * far[0, j, r, cols(h)].astype(F32) for t, h in zip(sums, some)
                )

            mix = mix_out[me, r].astype(F32)
            sums = tuple(spread(mix, HALF + h) * tk[r, cols(h)].astype(F32) for h in some)
            sums = lax.fori_loop(0, me, add_key, sums)
            for t, h in zip(sums, some):
                tdq[r, cols(h)] = (t * (sharp[1, h] * inv)).astype(BF16)

    def column_part(c):
        r = rows(c)

        @pl.loop(me + 1, frames)
        def _(i):
            remote(
                mix_out.at[me, r], mix_in.at[i, r], mix_send.at[me, c], mix_recv.at[i, c], "frame", mate
            ).wait_recv()

        for first in range(0, heads, HEADS_AT_ONCE):
            some = range(first, min(first + HEADS_AT_ONCE, heads))

            def add_row(i, sums):
                mix = mix_in[i, r].astype(F32)
                return tuple(
                    (
                        v + spread(mix, h) * far[1, i, r, cols(h)].astype(F32),
                        k + spread(mix, HALF + h) * far[0, i, r, cols(h)].astype(F32),
                    )
                    for (v, k), h in zip(sums, some)
                )

            mix = mix_out[me, r].astype(F32)
            sums = tuple(
                (
                    spread(mix, h) * tc[r, cols(h)].astype(F32),
                    spread(mix, HALF + h) * tq[r, cols(h)].astype(F32),
                )
                for h in some
            )
            sums = lax.fori_loop(me + 1, frames, add_row, sums)
            for (v, k), h in zip(sums, some):
                tdv[r, cols(h)] = v.astype(BF16)
                tdk[r, cols(h)] = (k * (sharp[1, h] * inv)).astype(BF16)

    def share(buffer, send, recv, axis, mine, size):
        for d in range(1, size):
            remote(
                buffer.at[mine], buffer.at[mine], send.at[d], recv.at[mine], axis, lax.rem(mine + d, size)
            ).start()

    def shared(buffer, send, recv, axis, mine, size):
        for d in range(1, size):
            slot = lax.rem(mine + d, size)
            remote(buffer.at[slot], buffer.at[slot], send.at[d], recv.at[slot], axis, slot).wait_recv()
        total = buffer[0]
        for i in range(1, size):
            total = total + buffer[i]
        return total

    per_step = -(-heads // CHUNKS)

    @pl.loop(0, CHUNKS)
    def _(c):
        for t in range(per_step):
            h = c * per_step + t
            if heads % CHUNKS == 0:
                spatial(h)
            else:
                pl.when(h < heads)(functools.partial(spatial, h))

        @pl.when(c >= 1)
        def _():
            row_part(c - 1)

        @pl.when(c >= 2)
        def _():
            column_part(c - 2)

        for part in range(2):
            for d in others:
                slot = chip_at(d) * 2 + core
                far_here(part, slot, c)
                far_copy(part, slot, c, far.at[part, slot], pass_send.at[part, d, c], mate).start()

    row_part(CHUNKS - 1)

    per_head = jnp.sum(logit_heads[...], axis=1, keepdims=True)
    tall = logit_heads.shape[0]
    own_lane = lax.broadcasted_iota(jnp.int32, (tall, LANES), 0) == lax.broadcasted_iota(
        jnp.int32, (tall, LANES), 1
    )
    spatial_sum = jnp.sum(jnp.where(own_lane, per_head, 0.0), axis=0, keepdims=True)
    temporal_sum = jnp.sum(logit_rows[...], axis=0, keepdims=True)
    which = lax.broadcasted_iota(jnp.int32, (8, LANES), 0)
    sum_frame[me] = jnp.where(which == 0, spatial_sum, jnp.where(which == 1, temporal_sum, 0.0))
    share(sum_frame, frame_send, frame_recv, "frame", me, frames)
    column_part(CHUNKS - 2)
    sum_clip[clip] = shared(sum_frame, frame_send, frame_recv, "frame", me, frames)
    share(sum_clip, clip_send, clip_recv, "clip", clip, clips)
    column_part(CHUNKS - 1)
    total = shared(sum_clip, clip_send, clip_recv, "clip", clip, clips)
    logit[...] = total[0:2, 0:heads] * scale_norm

    for d in range(1, frames):
        remote(sum_frame.at[me], sum_frame.at[me], frame_send.at[d], frame_recv.at[me], "frame", mate).wait_send()
    for d in range(1, clips):
        remote(sum_clip.at[clip], sum_clip.at[clip], clip_send.at[d], clip_recv.at[clip], "frame", mate).wait_send()

    @pl.loop(0, CHUNKS)
    def _(c):
        for part in range(2):
            far_copy(part, me, c, tq_in, mate_send.at[part, c], mate).wait_send()
            for d in others:
                far_copy(part, me, c, tq_in, cross_send.at[part, d, c], mate).wait_send()
                slot = chip_at(d) * 2 + core
                far_copy(part, slot, c, far.at[part, slot], pass_send.at[part, d, c], mate).wait_send()

        @pl.loop(0, me)
        def _(j):
            r = rows(c)
            remote(
                mix_out.at[j, r], mix_in.at[me, r], mix_send.at[j, c], mix_recv.at[me, c], "frame", mate
            ).wait_send()


def on_device(sq, sk, sv, sc, tq, tk, tv, tc, sharpness):
    frames, clips = lax.axis_size("frame"), lax.axis_size("clip")
    heads = sharpness.shape[1]
    full = sq.shape
    patches, features = full[2], full[3]
    block = patches // CHUNKS
    chips = frames // 2
    flat = [x.reshape(patches, features) for x in (sq, sk, sv, sc, tq, tk, tv, tc)]
    plane = jax.ShapeDtypeStruct((patches, features), BF16)
    scale_norm = 1.0 / math.sqrt(clips * full[0] * frames * full[1] * patches)
    dma = pltpu.SemaphoreType.DMA
    out = pl.pallas_call(
        functools.partial(kernel, frames, clips, heads, scale_norm),
        out_shape=(plane,) * 5 + (jax.ShapeDtypeStruct((2, heads), F32),),
        in_specs=[pl.BlockSpec(memory_space=pltpu.SMEM)] + [pl.BlockSpec(memory_space=pl.ANY)] * 8,
        out_specs=(pl.BlockSpec(memory_space=pltpu.VMEM),) * 6,
        scratch_shapes=[pltpu.VMEM((patches, features), BF16)] * 8
        + [
            pltpu.VMEM((2, frames, patches, features), BF16),
            pltpu.VMEM((frames, block, LANES), F32),
            pltpu.VMEM((frames, block, LANES), F32),
            pltpu.VMEM((frames, patches, LANES), BF16),
            pltpu.VMEM((frames, patches, LANES), BF16),
            pltpu.VMEM((block, LANES), F32),
            pltpu.VMEM((-(-heads // 8) * 8, patches), F32),
            pltpu.VMEM((frames, 8, LANES), F32),
            pltpu.VMEM((clips, 8, LANES), F32),
            dma((8,)),
            dma((2, chips, CHUNKS)),
            dma((2, CHUNKS)),
            dma((2, chips, CHUNKS)),
            dma((frames, CHUNKS)),
            dma((frames,)),
            dma((clips,)),
            dma((2, frames, CHUNKS)),
            dma((frames, CHUNKS)),
            dma((frames,)),
            dma((clips,)),
        ],
        compiler_params=pltpu.CompilerParams(
            collective_id=0, has_side_effects=True, vmem_limit_bytes=48 * 1024 * 1024
        ),
    )(sharpness, *flat)
    return tuple(x.reshape(full) for x in out[:5]) + (out[5],)


def solution(mesh):
    part = P("clip", "frame", None, None)
    return jax.shard_map(
        on_device,
        mesh=mesh,
        in_specs=(part,) * 8 + (P(),),
        out_specs=(part,) * 5 + (P(),),
        check_vma=False,
    )
```

```python
import functools
import math

import jax
import jax.numpy as jnp
from jax import lax
from jax.experimental import pallas as pl
from jax.experimental.pallas import tpu as pltpu
from jax.sharding import PartitionSpec as P

F32 = jnp.float32
BF16 = jnp.bfloat16
LANES = 128
HALF = 64
CHUNKS = 4
SPLIT = 2
AHEAD = 3
HEADS_AT_ONCE = 6


def contract(left, right, left_dim, right_dim):
    return lax.dot_general(
        left, right, (((left_dim,), (right_dim,)), ((), ())), preferred_element_type=F32
    )


def kernel(
    frames,
    clips,
    heads,
    scale_norm,
    sharp_in,
    sq_in,
    sk_in,
    sv_in,
    sc_in,
    tq_in,
    tk_in,
    tv_in,
    tc_in,
    sdq,
    sdk,
    tdq,
    tdk,
    tdv,
    logit,
    sharp,
    sq,
    sk,
    sv,
    sc,
    tq,
    tk,
    tv,
    tc,
    far,
    raw_s,
    grad_s,
    mix_out,
    mix_in,
    logit_rows,
    logit_heads,
    sum_frame,
    sum_clip,
    load_sem,
    cross_send,
    mate_send,
    pass_send,
    mix_send,
    frame_send,
    clip_send,
    far_recv,
    mix_recv,
    frame_recv,
    clip_recv,
):
    me = lax.axis_index("frame")
    clip = lax.axis_index("clip")
    chips = frames // 2
    chip, core = me // 2, lax.rem(me, 2)
    mate = chip * 2 + 1 - core
    patches, features = sq.shape
    width = features // heads
    block = patches // CHUNKS
    pieces = CHUNKS * SPLIT
    piece = block // SPLIT
    inv = 1.0 / math.sqrt(width)
    others = range(1, chips)

    def rows(c):
        return pl.ds(pl.multiple_of(c * block, block), block)

    def cols(h):
        return slice(h * width, (h + 1) * width)

    def remote(src, dst, send, recv, axis, target):
        return pltpu.make_async_remote_copy(
            src_ref=src,
            dst_ref=dst,
            send_sem=send,
            recv_sem=recv,
            device_id={axis: target},
            device_id_type=pl.DeviceIdType.MESH,
        )

    def piece_rows(p):
        return pl.ds(pl.multiple_of(p * piece, piece), piece)

    def far_copy(part, slot, r, at, src, send, target):
        return remote(src.at[r], far.at[part, slot, r], send, far_recv.at[part, slot, at], "frame", target)

    def far_here(part, slot, r, at):
        far_copy(part, slot, r, at, far.at[part, slot], mate_send.at[part, 0], mate).wait_recv()

    def chip_at(d):
        return lax.rem(chip + d, chips)

    loads = [
        pltpu.make_async_copy(src, dst, load_sem.at[i])
        for i, (src, dst) in enumerate(
            ((sharp_in, sharp), (sq_in, sq), (sk_in, sk), (sv_in, sv), (sc_in, sc), (tq_in, tq), (tk_in, tk), (tv_in, tv), (tc_in, tc))
        )
    ]
    for load in loads:
        load.start()

    barrier = pltpu.get_barrier_semaphore()
    for d in range(1, frames):
        pl.semaphore_signal(
            barrier, inc=1, device_id={"frame": lax.rem(me + d, frames)}, device_id_type=pl.DeviceIdType.MESH
        )
    for d in range(1, clips):
        pl.semaphore_signal(
            barrier, inc=1, device_id={"clip": lax.rem(clip + d, clips)}, device_id_type=pl.DeviceIdType.MESH
        )
    pl.semaphore_wait(barrier, frames + clips - 2)

    def send_to(target, r, at, sems):
        @pl.when(target < me)
        def _():
            far_copy(0, me, r, at, tq_in, sems(0), target).start()
            far_copy(1, me, r, at, tc_in, sems(1), target).start()

        @pl.when(target > me)
        def _():
            far_copy(0, me, r, at, tk_in, sems(0), target).start()
            far_copy(1, me, r, at, tv_in, sems(1), target).start()

    def send_far(p):
        for d in others:
            send_to(chip_at(d) * 2 + core, piece_rows(p), p, lambda part: cross_send.at[part, d, p])

    for p in range(AHEAD):
        send_far(p)
    for c in range(CHUNKS):
        send_to(mate, rows(c), c, lambda part: mate_send.at[part, c])

    raw_s[...] = jnp.zeros_like(raw_s)
    grad_s[...] = jnp.zeros_like(grad_s)
    logit_rows[...] = jnp.zeros_like(logit_rows)
    logit_heads[...] = jnp.zeros_like(logit_heads)
    for load in loads:
        load.wait()

    lane_row = lax.broadcasted_iota(jnp.int32, (1, LANES), 1)
    sharp_lanes = jnp.zeros((1, LANES), F32)
    for h in range(heads):
        sharp_lanes = jnp.where(lane_row == h, sharp[1, h], sharp_lanes)
    lane = lax.broadcasted_iota(jnp.int32, (block, LANES), 1)
    place = jnp.full((block, LANES), me, jnp.int32)

    def spatial(h):
        at = pl.ds(pl.multiple_of(h * width, width), width)
        query, key, value, cotangent = sq[:, at], sk[:, at], sv[:, at], sc[:, at]
        sharpness = sharp[0, h]
        raw = contract(query, key, 1, 1) * inv
        scores = raw * sharpness
        exponent = jnp.exp(scores - jnp.max(scores, axis=1, keepdims=True))
        weights = exponent * (1.0 / jnp.sum(exponent, axis=1, keepdims=True))
        weight_grad = contract(cotangent, value, 1, 1)
        delta = jnp.sum(weights * weight_grad, axis=1, keepdims=True)
        score_grad = weights * (weight_grad - delta)
        low = score_grad.astype(BF16)
        factor = sharpness * inv
        sdq[:, at] = (contract(low, key, 1, 0) * factor).astype(BF16)
        sdk[:, at] = (contract(low, query, 0, 0) * factor).astype(BF16)
        logit_heads[pl.ds(h, 1), :] = jnp.sum(score_grad * raw, axis=0, keepdims=True)

    def dots(left, right):
        out = jnp.zeros((block, LANES), F32)
        for h in range(heads):
            product = left(cols(h)).astype(F32) * right(cols(h)).astype(F32)
            out = jnp.where(lane == h, jnp.sum(product, axis=1, keepdims=True), out)
        return out

    def spread(mix, at):
        return jnp.broadcast_to(mix[:, at : at + 1], (block, width))

    def row_part(c):
        r = rows(c)
        for part in range(2):
            far_here(part, mate, r, c)
            for d in others:
                for p in range(SPLIT):
                    far_here(part, chip_at(d) * 2 + 1 - core, piece_rows(c * SPLIT + p), c * SPLIT + p)
        raw_own = dots(lambda s: tq[r, s], lambda s: tk[r, s]) * inv
        grad_own = dots(lambda s: tc[r, s], lambda s: tv[r, s])

        @pl.loop(0, me)
        def _(j):
            raw_s[j] = dots(lambda s: tq[r, s], lambda s: far[0, j, r, s]) * inv
            grad_s[j] = dots(lambda s: tc[r, s], lambda s: far[1, j, r, s])

        scores_own = raw_own * sharp_lanes
        raw = [raw_s[j] for j in range(frames - 1)]
        grad = [grad_s[j] for j in range(frames - 1)]
        scores = [x * sharp_lanes for x in raw]
        top = scores_own
        for j, x in enumerate(scores):
            top = jnp.maximum(top, jnp.where(place > j, x, scores_own))
        exponent_own = jnp.exp(scores_own - top)
        exponent = [jnp.where(place > j, jnp.exp(x - top), 0.0) for j, x in enumerate(scores)]
        total, mean = exponent_own, exponent_own * grad_own
        for e, g in zip(exponent, grad):
            total, mean = total + e, mean + e * g
        over = 1.0 / total
        delta = mean * over

        def mixed(e, g):
            weights = e * over
            score_grad = weights * (g - delta)
            return score_grad, jnp.where(lane < HALF, weights, pltpu.roll(score_grad, HALF, 1)).astype(BF16)

        score_grad, mix = mixed(exponent_own, grad_own)
        mix_out[me, r] = mix
        share_sum = score_grad * raw_own

        for j in range(frames - 1):
            score_grad, mix = mixed(exponent[j], grad[j])
            share_sum = share_sum + score_grad * raw[j]

            def send_mix(j=j, mix=mix):
                mix_out[j, r] = mix
                remote(
                    mix_out.at[j, r], mix_in.at[me, r], mix_send.at[j, c], mix_recv.at[me, c], "frame", j
                ).start()

            pl.when(j < me)(send_mix)

        logit_rows[...] += share_sum

        for first in range(0, heads, HEADS_AT_ONCE):
            some = range(first, min(first + HEADS_AT_ONCE, heads))

            def add_key(j, sums):
                mix = mix_out[j, r].astype(F32)
                return tuple(
                    t + spread(mix, HALF + h) * far[0, j, r, cols(h)].astype(F32) for t, h in zip(sums, some)
                )

            mix = mix_out[me, r].astype(F32)
            sums = tuple(spread(mix, HALF + h) * tk[r, cols(h)].astype(F32) for h in some)
            sums = lax.fori_loop(0, me, add_key, sums)
            for t, h in zip(sums, some):
                tdq[r, cols(h)] = (t * (sharp[1, h] * inv)).astype(BF16)

    def column_part(c):
        r = rows(c)

        @pl.loop(me + 1, frames)
        def _(i):
            remote(
                mix_out.at[me, r], mix_in.at[i, r], mix_send.at[me, c], mix_recv.at[i, c], "frame", mate
            ).wait_recv()

        for first in range(0, heads, HEADS_AT_ONCE):
            some = range(first, min(first + HEADS_AT_ONCE, heads))

            def add_row(i, sums):
                mix = mix_in[i, r].astype(F32)
                return tuple(
                    (
                        v + spread(mix, h) * far[1, i, r, cols(h)].astype(F32),
                        k + spread(mix, HALF + h) * far[0, i, r, cols(h)].astype(F32),
                    )
                    for (v, k), h in zip(sums, some)
                )

            mix = mix_out[me, r].astype(F32)
            sums = tuple(
                (
                    spread(mix, h) * tc[r, cols(h)].astype(F32),
                    spread(mix, HALF + h) * tq[r, cols(h)].astype(F32),
                )
                for h in some
            )
            sums = lax.fori_loop(me + 1, frames, add_row, sums)
            for (v, k), h in zip(sums, some):
                tdv[r, cols(h)] = v.astype(BF16)
                tdk[r, cols(h)] = (k * (sharp[1, h] * inv)).astype(BF16)

    def share(buffer, send, recv, axis, mine, size):
        for d in range(1, size):
            remote(
                buffer.at[mine], buffer.at[mine], send.at[d], recv.at[mine], axis, lax.rem(mine + d, size)
            ).start()

    def shared(buffer, send, recv, axis, mine, size):
        for d in range(1, size):
            slot = lax.rem(mine + d, size)
            remote(buffer.at[slot], buffer.at[slot], send.at[d], recv.at[slot], axis, slot).wait_recv()
        total = buffer[0]
        for i in range(1, size):
            total = total + buffer[i]
        return total

    def take(p):
        for part in range(2):
            for d in others:
                slot = chip_at(d) * 2 + core
                far_here(part, slot, piece_rows(p), p)
                far_copy(
                    part, slot, piece_rows(p), p, far.at[part, slot], pass_send.at[part, d, p], mate
                ).start()

        @pl.when(p + AHEAD < pieces)
        def _():
            send_far(p + AHEAD)

    per_step = -(-heads // CHUNKS)

    @pl.loop(0, CHUNKS)
    def _(c):
        for t in range(per_step):
            h = c * per_step + t
            if heads % CHUNKS == 0:
                spatial(h)
            else:
                pl.when(h < heads)(functools.partial(spatial, h))

        take(c * SPLIT)

        @pl.when(c >= 1)
        def _():
            row_part(c - 1)

        @pl.when(c >= 2)
        def _():
            column_part(c - 2)

        take(c * SPLIT + 1)

    row_part(CHUNKS - 1)

    per_head = jnp.sum(logit_heads[...], axis=1, keepdims=True)
    tall = logit_heads.shape[0]
    own_lane = lax.broadcasted_iota(jnp.int32, (tall, LANES), 0) == lax.broadcasted_iota(
        jnp.int32, (tall, LANES), 1
    )
    spatial_sum = jnp.sum(jnp.where(own_lane, per_head, 0.0), axis=0, keepdims=True)
    temporal_sum = jnp.sum(logit_rows[...], axis=0, keepdims=True)
    which = lax.broadcasted_iota(jnp.int32, (8, LANES), 0)
    sum_frame[me] = jnp.where(which == 0, spatial_sum, jnp.where(which == 1, temporal_sum, 0.0))
    share(sum_frame, frame_send, frame_recv, "frame", me, frames)
    column_part(CHUNKS - 2)
    sum_clip[clip] = shared(sum_frame, frame_send, frame_recv, "frame", me, frames)
    share(sum_clip, clip_send, clip_recv, "clip", clip, clips)
    column_part(CHUNKS - 1)
    total = shared(sum_clip, clip_send, clip_recv, "clip", clip, clips)
    logit[...] = total[0:2, 0:heads] * scale_norm

    for d in range(1, frames):
        remote(sum_frame.at[me], sum_frame.at[me], frame_send.at[d], frame_recv.at[me], "frame", mate).wait_send()
    for d in range(1, clips):
        remote(sum_clip.at[clip], sum_clip.at[clip], clip_send.at[d], clip_recv.at[clip], "frame", mate).wait_send()

    @pl.loop(0, CHUNKS)
    def _(c):
        for part in range(2):
            far_copy(part, me, rows(c), c, tq_in, mate_send.at[part, c], mate).wait_send()

        @pl.loop(0, me)
        def _(j):
            r = rows(c)
            remote(
                mix_out.at[j, r], mix_in.at[me, r], mix_send.at[j, c], mix_recv.at[me, c], "frame", mate
            ).wait_send()


    @pl.loop(0, pieces)
    def _(p):
        for part in range(2):
            for d in others:
                slot, r = chip_at(d) * 2 + core, piece_rows(p)
                far_copy(part, me, r, p, tq_in, cross_send.at[part, d, p], mate).wait_send()
                far_copy(part, slot, r, p, far.at[part, slot], pass_send.at[part, d, p], mate).wait_send()


def store_kernel(*refs):
    count = len(refs) // 2
    copies = [
        pltpu.make_async_copy(refs[i], refs[count + i], refs[-1].at[i]) for i in range(count)
    ]
    for copy in copies:
        copy.start()
    for copy in copies:
        copy.wait()


def on_device(sq, sk, sv, sc, tq, tk, tv, tc, sharpness):
    frames, clips = lax.axis_size("frame"), lax.axis_size("clip")
    heads = sharpness.shape[1]
    full = sq.shape
    patches, features = full[2], full[3]
    block = patches // CHUNKS
    chips = frames // 2
    flat = [x.reshape(patches, features) for x in (sq, sk, sv, sc, tq, tk, tv, tc)]
    plane = jax.ShapeDtypeStruct((patches, features), BF16)
    scale_norm = 1.0 / math.sqrt(clips * full[0] * frames * full[1] * patches)
    dma = pltpu.SemaphoreType.DMA
    out = pl.pallas_call(
        functools.partial(kernel, frames, clips, heads, scale_norm),
        out_shape=(plane,) * 5 + (jax.ShapeDtypeStruct((2, heads), F32),),
        in_specs=[pl.BlockSpec(memory_space=pltpu.HBM)] * 9,
        out_specs=(pl.BlockSpec(memory_space=pltpu.VMEM),) * 6,
        scratch_shapes=[pltpu.SMEM((2, heads), F32)]
        + [pltpu.VMEM((patches, features), BF16)] * 8
        + [
            pltpu.VMEM((2, frames, patches, features), BF16),
            pltpu.VMEM((frames, block, LANES), F32),
            pltpu.VMEM((frames, block, LANES), F32),
            pltpu.VMEM((frames, patches, LANES), BF16),
            pltpu.VMEM((frames, patches, LANES), BF16),
            pltpu.VMEM((block, LANES), F32),
            pltpu.VMEM((-(-heads // 8) * 8, patches), F32),
            pltpu.VMEM((frames, 8, LANES), F32),
            pltpu.VMEM((clips, 8, LANES), F32),
            dma((9,)),
            dma((2, chips, CHUNKS * SPLIT)),
            dma((2, CHUNKS)),
            dma((2, chips, CHUNKS * SPLIT)),
            dma((frames, CHUNKS)),
            dma((frames,)),
            dma((clips,)),
            dma((2, frames, CHUNKS * SPLIT)),
            dma((frames, CHUNKS)),
            dma((frames,)),
            dma((clips,)),
        ],
        compiler_params=pltpu.CompilerParams(
            collective_id=0, has_side_effects=True, vmem_limit_bytes=32 * 1024 * 1024
        ),
    )(sharpness, *flat)
    out = pl.pallas_call(
        store_kernel,
        out_shape=(plane,) * 5 + (jax.ShapeDtypeStruct((2, heads), F32),),
        in_specs=[pl.BlockSpec(memory_space=pltpu.VMEM)] * 6,
        out_specs=(pl.BlockSpec(memory_space=pltpu.HBM),) * 6,
        scratch_shapes=[dma((6,))],
    )(*out)
    return tuple(x.reshape(full) for x in out[:5]) + (out[5],)


def solution(mesh):
    part = P("clip", "frame", None, None)
    return jax.shard_map(
        on_device,
        mesh=mesh,
        in_specs=(part,) * 8 + (P(),),
        out_specs=(part,) * 5 + (P(),),
        check_vma=False,
    )
```

```python
import functools
import math

import jax
import jax.numpy as jnp
from jax import lax
from jax.experimental import pallas as pl
from jax.experimental.pallas import tpu as pltpu
from jax.sharding import PartitionSpec as P

F32 = jnp.float32
BF16 = jnp.bfloat16
LANES = 128
HALF = 64
CHUNKS = 4
SPLIT = 2
AHEAD = 3
HEADS_AT_ONCE = 6
WRITTEN_OUT = 4
OUTPUTS = 5
GRANT = 61 * 1024 * 1024


def contract(left, right, left_dim, right_dim):
    return lax.dot_general(
        left, right, (((left_dim,), (right_dim,)), ((), ())), preferred_element_type=F32
    )


def kernel(
    frames,
    clips,
    heads,
    scale_norm,
    sharp_in,
    sq_in,
    sk_in,
    sv_in,
    sc_in,
    tq_in,
    tk_in,
    tv_in,
    tc_in,
    sdq_out,
    sdk_out,
    tdq_out,
    tdk_out,
    tdv_out,
    logit,
    sharp,
    sq,
    sk,
    sv,
    sc,
    tq,
    tk,
    tv,
    tc,
    sdq,
    sdk,
    tdq,
    tdk,
    tdv,
    far,
    raw_s,
    grad_s,
    mix_out,
    mix_in,
    logit_rows,
    logit_heads,
    sum_frame,
    sum_clip,
    load_sem,
    spatial_sem,
    store_sem,
    cross_send,
    mate_send,
    pass_send,
    mix_send,
    frame_send,
    clip_send,
    far_recv,
    mix_recv,
    frame_recv,
    clip_recv,
):
    me = lax.axis_index("frame")
    clip = lax.axis_index("clip")
    chips = frames // 2
    chip, core = me // 2, lax.rem(me, 2)
    mate = chip * 2 + 1 - core
    patches, features = sq.shape
    width = features // heads
    block = patches // CHUNKS
    pieces = CHUNKS * SPLIT
    piece = block // SPLIT
    inv = 1.0 / math.sqrt(width)
    others = range(1, chips)

    def rows(c):
        return pl.ds(pl.multiple_of(c * block, block), block)

    def cols(h):
        return slice(h * width, (h + 1) * width)

    def remote(src, dst, send, recv, axis, target):
        return pltpu.make_async_remote_copy(
            src_ref=src,
            dst_ref=dst,
            send_sem=send,
            recv_sem=recv,
            device_id={axis: target},
            device_id_type=pl.DeviceIdType.MESH,
        )

    def piece_rows(p):
        return pl.ds(pl.multiple_of(p * piece, piece), piece)

    def far_copy(part, slot, r, at, src, send, target):
        return remote(src.at[r], far.at[part, slot, r], send, far_recv.at[part, slot, at], "frame", target)

    def far_here(part, slot, r, at):
        far_copy(part, slot, r, at, far.at[part, slot], mate_send.at[part, 0], mate).wait_recv()

    def chip_at(d):
        return lax.rem(chip + d, chips)

    loads = [
        pltpu.make_async_copy(src, dst, load_sem.at[i])
        for i, (src, dst) in enumerate(
            ((sharp_in, sharp), (sq_in, sq), (sk_in, sk), (sv_in, sv), (sc_in, sc), (tq_in, tq), (tk_in, tk), (tv_in, tv), (tc_in, tc))
        )
    ]
    for load in loads:
        load.start()

    barrier = pltpu.get_barrier_semaphore()
    for d in range(1, frames):
        pl.semaphore_signal(
            barrier, inc=1, device_id={"frame": lax.rem(me + d, frames)}, device_id_type=pl.DeviceIdType.MESH
        )
    for d in range(1, clips):
        pl.semaphore_signal(
            barrier, inc=1, device_id={"clip": lax.rem(clip + d, clips)}, device_id_type=pl.DeviceIdType.MESH
        )
    pl.semaphore_wait(barrier, frames + clips - 2)

    def send_to(target, r, at, sems):
        @pl.when(target < me)
        def _():
            far_copy(0, me, r, at, tq_in, sems(0), target).start()
            far_copy(1, me, r, at, tc_in, sems(1), target).start()

        @pl.when(target > me)
        def _():
            far_copy(0, me, r, at, tk_in, sems(0), target).start()
            far_copy(1, me, r, at, tv_in, sems(1), target).start()

    def send_far(p):
        for d in others:
            send_to(chip_at(d) * 2 + core, piece_rows(p), p, lambda part: cross_send.at[part, d, p])

    for p in range(AHEAD):
        send_far(p)
    for c in range(CHUNKS):
        send_to(mate, rows(c), c, lambda part: mate_send.at[part, c])

    raw_s[...] = jnp.zeros_like(raw_s)
    grad_s[...] = jnp.zeros_like(grad_s)
    logit_rows[...] = jnp.zeros_like(logit_rows)
    logit_heads[...] = jnp.zeros_like(logit_heads)
    for load in loads:
        load.wait()

    lane_row = lax.broadcasted_iota(jnp.int32, (1, LANES), 1)
    sharp_lanes = jnp.zeros((1, LANES), F32)
    for h in range(heads):
        sharp_lanes = jnp.where(lane_row == h, sharp[1, h], sharp_lanes)
    lane = lax.broadcasted_iota(jnp.int32, (block, LANES), 1)
    place = jnp.full((block, LANES), me, jnp.int32)

    def spatial(h):
        at = pl.ds(pl.multiple_of(h * width, width), width)
        query, key, value, cotangent = sq[:, at], sk[:, at], sv[:, at], sc[:, at]
        sharpness = sharp[0, h]
        raw = contract(query, key, 1, 1) * inv
        scores = raw * sharpness
        exponent = jnp.exp(scores - jnp.max(scores, axis=1, keepdims=True))
        weights = exponent * (1.0 / jnp.sum(exponent, axis=1, keepdims=True))
        weight_grad = contract(cotangent, value, 1, 1)
        delta = jnp.sum(weights * weight_grad, axis=1, keepdims=True)
        score_grad = weights * (weight_grad - delta)
        low = score_grad.astype(BF16)
        factor = sharpness * inv
        sdq[:, at] = (contract(low, key, 1, 0) * factor).astype(BF16)
        sdk[:, at] = (contract(low, query, 0, 0) * factor).astype(BF16)
        logit_heads[pl.ds(h, 1), :] = jnp.sum(score_grad * raw, axis=0, keepdims=True)

    def dots(left, right):
        out = jnp.zeros((block, LANES), F32)
        for h in range(heads):
            product = left(cols(h)).astype(F32) * right(cols(h)).astype(F32)
            out = jnp.where(lane == h, jnp.sum(product, axis=1, keepdims=True), out)
        return out

    def spread(mix, at):
        return jnp.broadcast_to(mix[:, at : at + 1], (block, width))

    def fold(low, high, body, start):
        if isinstance(low, int) and isinstance(high, int):
            for i in range(low, high):
                start = body(i, start)
            return start
        return lax.fori_loop(low, high, body, start)

    def store(which, c):
        src, dst = ((tdq, tdq_out), (tdk, tdk_out), (tdv, tdv_out))[which]
        return pltpu.make_async_copy(src.at[rows(c)], dst.at[rows(c)], store_sem.at[which, c])

    def row_part(c, own):
        r = rows(c)
        known = isinstance(own, int)
        for part in range(2):
            far_here(part, mate, r, c)
            for d in others:
                for p in range(SPLIT):
                    far_here(part, chip_at(d) * 2 + 1 - core, piece_rows(c * SPLIT + p), c * SPLIT + p)
        raw_own = dots(lambda s: tq[r, s], lambda s: tk[r, s]) * inv
        grad_own = dots(lambda s: tc[r, s], lambda s: tv[r, s])

        def pair(j):
            return (
                dots(lambda s: tq[r, s], lambda s: far[0, j, r, s]) * inv,
                dots(lambda s: tc[r, s], lambda s: far[1, j, r, s]),
            )

        if known:
            pairs = [pair(j) for j in range(own)]
        else:

            @pl.loop(0, own)
            def _(j):
                raw_s[j], grad_s[j] = pair(j)

            pairs = [(raw_s[j], grad_s[j]) for j in range(frames - 1)]

        def seen(j, x, other):
            return x if known else jnp.where(place > j, x, other)

        scores_own = raw_own * sharp_lanes
        scores = [x * sharp_lanes for x, _ in pairs]
        top = scores_own
        for j, x in enumerate(scores):
            top = jnp.maximum(top, seen(j, x, scores_own))
        exponent_own = jnp.exp(scores_own - top)
        exponent = [seen(j, jnp.exp(x - top), 0.0) for j, x in enumerate(scores)]
        total, mean = exponent_own, exponent_own * grad_own
        for e, (_, g) in zip(exponent, pairs):
            total, mean = total + e, mean + e * g
        over = 1.0 / total
        delta = mean * over

        def mixed(e, g):
            weights = e * over
            score_grad = weights * (g - delta)
            return score_grad, jnp.where(lane < HALF, weights, pltpu.roll(score_grad, HALF, 1)).astype(BF16)

        score_grad, mix_own = mixed(exponent_own, grad_own)
        mix_out[own, r] = mix_own
        share_sum = score_grad * raw_own

        for j, (raw, grad) in enumerate(pairs):
            score_grad, mix = mixed(exponent[j], grad)
            share_sum = share_sum + score_grad * raw

            def send_mix(j=j, mix=mix):
                mix_out[j, r] = mix
                remote(
                    mix_out.at[j, r], mix_in.at[me, r], mix_send.at[j, c], mix_recv.at[me, c], "frame", j
                ).start()

            if known:
                send_mix()
            else:
                pl.when(j < own)(send_mix)

        logit_rows[...] += share_sum

        for first in range(0, heads, HEADS_AT_ONCE):
            some = range(first, min(first + HEADS_AT_ONCE, heads))

            def add_key(j, sums):
                mix = mix_out[j, r].astype(F32)
                return tuple(
                    t + spread(mix, HALF + h) * far[0, j, r, cols(h)].astype(F32) for t, h in zip(sums, some)
                )

            mix = mix_own.astype(F32)
            sums = tuple(spread(mix, HALF + h) * tk[r, cols(h)].astype(F32) for h in some)
            sums = fold(0, own, add_key, sums)
            for t, h in zip(sums, some):
                tdq[r, cols(h)] = (t * (sharp[1, h] * inv)).astype(BF16)
        store(0, c).start()

    def column_part(c, own):
        r = rows(c)

        def arrived(i, carry):
            remote(
                mix_out.at[me, r], mix_in.at[i, r], mix_send.at[me, c], mix_recv.at[i, c], "frame", mate
            ).wait_recv()
            return carry

        fold(own + 1, frames, arrived, 0)

        for first in range(0, heads, HEADS_AT_ONCE):
            some = range(first, min(first + HEADS_AT_ONCE, heads))

            def add_row(i, sums):
                mix = mix_in[i, r].astype(F32)
                return tuple(
                    (
                        v + spread(mix, h) * far[1, i, r, cols(h)].astype(F32),
                        k + spread(mix, HALF + h) * far[0, i, r, cols(h)].astype(F32),
                    )
                    for (v, k), h in zip(sums, some)
                )

            mix = mix_out[own, r].astype(F32)
            sums = tuple(
                (
                    spread(mix, h) * tc[r, cols(h)].astype(F32),
                    spread(mix, HALF + h) * tq[r, cols(h)].astype(F32),
                )
                for h in some
            )
            sums = fold(own + 1, frames, add_row, sums)
            for (v, k), h in zip(sums, some):
                tdv[r, cols(h)] = v.astype(BF16)
                tdk[r, cols(h)] = (k * (sharp[1, h] * inv)).astype(BF16)
        store(1, c).start()
        store(2, c).start()

    def as_frame(work, c):
        if frames > WRITTEN_OUT:
            work(c, me)
            return
        for f in range(frames):
            pl.when(me == f)(functools.partial(work, c, f))

    def share(buffer, send, recv, axis, mine, size):
        for d in range(1, size):
            remote(
                buffer.at[mine], buffer.at[mine], send.at[d], recv.at[mine], axis, lax.rem(mine + d, size)
            ).start()

    def shared(buffer, send, recv, axis, mine, size):
        for d in range(1, size):
            slot = lax.rem(mine + d, size)
            remote(buffer.at[slot], buffer.at[slot], send.at[d], recv.at[slot], axis, slot).wait_recv()
        total = buffer[0]
        for i in range(1, size):
            total = total + buffer[i]
        return total

    def take(p):
        for part in range(2):
            for d in others:
                slot = chip_at(d) * 2 + core
                far_here(part, slot, piece_rows(p), p)
                far_copy(
                    part, slot, piece_rows(p), p, far.at[part, slot], pass_send.at[part, d, p], mate
                ).start()

        @pl.when(p + AHEAD < pieces)
        def _():
            send_far(p + AHEAD)

    per_step = -(-heads // CHUNKS)

    def spatial_stores():
        return [
            pltpu.make_async_copy(src, dst, spatial_sem.at[i])
            for i, (src, dst) in enumerate(((sdq, sdq_out), (sdk, sdk_out)))
        ]

    def sum_here():
        per_head = jnp.sum(logit_heads[...], axis=1, keepdims=True)
        tall = logit_heads.shape[0]
        own_lane = lax.broadcasted_iota(jnp.int32, (tall, LANES), 0) == lax.broadcasted_iota(
            jnp.int32, (tall, LANES), 1
        )
        spatial_sum = jnp.sum(jnp.where(own_lane, per_head, 0.0), axis=0, keepdims=True)
        temporal_sum = jnp.sum(logit_rows[...], axis=0, keepdims=True)
        which = lax.broadcasted_iota(jnp.int32, (8, LANES), 0)
        sum_frame[me] = jnp.where(which == 0, spatial_sum, jnp.where(which == 1, temporal_sum, 0.0))
        share(sum_frame, frame_send, frame_recv, "frame", me, frames)

    def sum_frames():
        sum_clip[clip] = shared(sum_frame, frame_send, frame_recv, "frame", me, frames)
        share(sum_clip, clip_send, clip_recv, "clip", clip, clips)

    @pl.loop(0, CHUNKS + 2)
    def _(c):
        @pl.when(c < CHUNKS)
        def _():
            for t in range(per_step):
                h = c * per_step + t
                if heads % CHUNKS == 0:
                    spatial(h)
                else:
                    pl.when(h < heads)(functools.partial(spatial, h))
            take(c * SPLIT)

        @pl.when(c == CHUNKS - 1)
        def _():
            for copy in spatial_stores():
                copy.start()

        @pl.when((c >= 1) & (c <= CHUNKS))
        def _():
            as_frame(row_part, c - 1)

        pl.when(c == CHUNKS)(sum_here)
        pl.when(c == CHUNKS + 1)(sum_frames)

        @pl.when(c >= 2)
        def _():
            as_frame(column_part, c - 2)

        @pl.when(c < CHUNKS)
        def _():
            for p in range(1, SPLIT):
                take(c * SPLIT + p)

    total = shared(sum_clip, clip_send, clip_recv, "clip", clip, clips)
    logit[...] = total[0:2, 0:heads] * scale_norm

    for copy in spatial_stores():
        copy.wait()
    for d in range(1, frames):
        remote(sum_frame.at[me], sum_frame.at[me], frame_send.at[d], frame_recv.at[me], "frame", mate).wait_send()
    for d in range(1, clips):
        remote(sum_clip.at[clip], sum_clip.at[clip], clip_send.at[d], clip_recv.at[clip], "frame", mate).wait_send()

    @pl.loop(0, CHUNKS)
    def _(c):
        for part in range(2):
            far_copy(part, me, rows(c), c, tq_in, mate_send.at[part, c], mate).wait_send()

        for which in range(3):
            store(which, c).wait()

        @pl.loop(0, me)
        def _(j):
            r = rows(c)
            remote(
                mix_out.at[j, r], mix_in.at[me, r], mix_send.at[j, c], mix_recv.at[me, c], "frame", mate
            ).wait_send()


    @pl.loop(0, pieces)
    def _(p):
        for part in range(2):
            for d in others:
                slot, r = chip_at(d) * 2 + core, piece_rows(p)
                far_copy(part, me, r, p, tq_in, cross_send.at[part, d, p], mate).wait_send()
                far_copy(part, slot, r, p, far.at[part, slot], pass_send.at[part, d, p], mate).wait_send()


def store_kernel(*refs):
    count = len(refs) // 2
    sems = refs[-1]
    copies = []
    for i in range(count):
        src, dst = refs[i], refs[count + i]
        cuts = 2 if src.shape[0] % 32 == 0 else 1
        tall = src.shape[0] // cuts
        for part in range(cuts):
            r = pl.ds(part * tall, tall)
            copies.append(pltpu.make_async_copy(src.at[r], dst.at[r], sems.at[i, part]))
    for copy in copies:
        copy.start()
    for copy in copies:
        copy.wait()


def on_device(sq, sk, sv, sc, tq, tk, tv, tc, sharpness):
    frames, clips = lax.axis_size("frame"), lax.axis_size("clip")
    heads = sharpness.shape[1]
    full = sq.shape
    patches, features = full[2], full[3]
    block = patches // CHUNKS
    chips = frames // 2
    flat = [x.reshape(patches, features) for x in (sq, sk, sv, sc, tq, tk, tv, tc)]
    plane = jax.ShapeDtypeStruct((patches, features), BF16)
    scale_norm = 1.0 / math.sqrt(clips * full[0] * frames * full[1] * patches)
    dma = pltpu.SemaphoreType.DMA
    out = pl.pallas_call(
        functools.partial(kernel, frames, clips, heads, scale_norm),
        out_shape=(plane,) * 5 + (jax.ShapeDtypeStruct((2, heads), F32),),
        in_specs=[pl.BlockSpec(memory_space=pltpu.HBM)] * 9,
        out_specs=(pl.BlockSpec(memory_space=pltpu.HBM),) * OUTPUTS + (pl.BlockSpec(memory_space=pltpu.VMEM),),
        scratch_shapes=[pltpu.SMEM((2, heads), F32)]
        + [pltpu.VMEM((patches, features), BF16)] * (8 + OUTPUTS)
        + [
            pltpu.VMEM((2, frames, patches, features), BF16),
            pltpu.VMEM((frames, block, LANES), F32),
            pltpu.VMEM((frames, block, LANES), F32),
            pltpu.VMEM((frames, patches, LANES), BF16),
            pltpu.VMEM((frames, patches, LANES), BF16),
            pltpu.VMEM((block, LANES), F32),
            pltpu.VMEM((-(-heads // 8) * 8, patches), F32),
            pltpu.VMEM((frames, 8, LANES), F32),
            pltpu.VMEM((clips, 8, LANES), F32),
            dma((9,)),
            dma((2,)),
            dma((3, CHUNKS)),
            dma((2, chips, CHUNKS * SPLIT)),
            dma((2, CHUNKS)),
            dma((2, chips, CHUNKS * SPLIT)),
            dma((frames, CHUNKS)),
            dma((frames,)),
            dma((clips,)),
            dma((2, frames, CHUNKS * SPLIT)),
            dma((frames, CHUNKS)),
            dma((frames,)),
            dma((clips,)),
        ],
        compiler_params=pltpu.CompilerParams(
            collective_id=0, has_side_effects=True, vmem_limit_bytes=GRANT
        ),
    )(sharpness, *flat)
    out = pl.pallas_call(
        store_kernel,
        out_shape=(plane,) * 5 + (jax.ShapeDtypeStruct((2, heads), F32),),
        in_specs=[pl.BlockSpec(memory_space=pltpu.HBM)] * 6,
        out_specs=(pl.BlockSpec(memory_space=pltpu.HBM),) * 6,
        scratch_shapes=[dma((6, 2))],
        compiler_params=pltpu.CompilerParams(vmem_limit_bytes=GRANT),
    )(*out)
    return tuple(x.reshape(full) for x in out[:5]) + (out[5],)


def solution(mesh):
    part = P("clip", "frame", None, None)
    return jax.shard_map(
        on_device,
        mesh=mesh,
        in_specs=(part,) * 8 + (P(),),
        out_specs=(part,) * 5 + (P(),),
        check_vma=False,
    )
```

```python
import functools
import math

import jax
import jax.numpy as jnp
from jax import lax
from jax.experimental import pallas as pl
from jax.experimental.pallas import tpu as pltpu
from jax.sharding import PartitionSpec as P

F32 = jnp.float32
BF16 = jnp.bfloat16
LANES = 128
HALF = 64
CHUNKS = 4
SPLIT = 2
AHEAD = 8
HEADS_AT_ONCE = 6
WRITTEN_OUT = 4
OUTPUTS = 5
GRANT = 61 * 1024 * 1024


def contract(left, right, left_dim, right_dim):
    return lax.dot_general(
        left, right, (((left_dim,), (right_dim,)), ((), ())), preferred_element_type=F32
    )


def kernel(
    frames,
    clips,
    heads,
    scale_norm,
    sharp_in,
    sq_in,
    sk_in,
    sv_in,
    sc_in,
    tq_in,
    tk_in,
    tv_in,
    tc_in,
    sdq_out,
    sdk_out,
    tdq_out,
    tdk_out,
    tdv_out,
    logit,
    sharp,
    sq,
    sk,
    sv,
    sc,
    tq,
    tk,
    tv,
    tc,
    sdq,
    sdk,
    tdq,
    tdk,
    tdv,
    far,
    raw_s,
    grad_s,
    mix_out,
    mix_in,
    logit_rows,
    logit_heads,
    sum_frame,
    sum_clip,
    load_sem,
    spatial_sem,
    store_sem,
    cross_send,
    mate_send,
    pass_send,
    mix_send,
    frame_send,
    clip_send,
    far_recv,
    mix_recv,
    frame_recv,
    clip_recv,
):
    me = lax.axis_index("frame")
    clip = lax.axis_index("clip")
    chips = frames // 2
    chip, core = me // 2, lax.rem(me, 2)
    mate = chip * 2 + 1 - core
    patches, features = sq.shape
    width = features // heads
    block = patches // CHUNKS
    pieces = CHUNKS * SPLIT
    piece = block // SPLIT
    inv = 1.0 / math.sqrt(width)
    others = range(1, chips)

    def rows(c):
        return pl.ds(pl.multiple_of(c * block, block), block)

    def cols(h):
        return slice(h * width, (h + 1) * width)

    def remote(src, dst, send, recv, axis, target):
        return pltpu.make_async_remote_copy(
            src_ref=src,
            dst_ref=dst,
            send_sem=send,
            recv_sem=recv,
            device_id={axis: target},
            device_id_type=pl.DeviceIdType.MESH,
        )

    def piece_rows(p):
        return pl.ds(pl.multiple_of(p * piece, piece), piece)

    def far_copy(part, slot, r, at, src, send, target):
        return remote(src.at[r], far.at[part, slot, r], send, far_recv.at[part, slot, at], "frame", target)

    def far_here(part, slot, r, at):
        far_copy(part, slot, r, at, far.at[part, slot], mate_send.at[part, 0], mate).wait_recv()

    def chip_at(d):
        return lax.rem(chip + d, chips)

    loads = [
        pltpu.make_async_copy(src, dst, load_sem.at[i])
        for i, (src, dst) in enumerate(
            ((sharp_in, sharp), (sq_in, sq), (sk_in, sk), (sv_in, sv), (sc_in, sc), (tq_in, tq), (tk_in, tk), (tv_in, tv), (tc_in, tc))
        )
    ]
    for load in loads:
        load.start()

    barrier = pltpu.get_barrier_semaphore()
    for d in range(1, frames):
        pl.semaphore_signal(
            barrier, inc=1, device_id={"frame": lax.rem(me + d, frames)}, device_id_type=pl.DeviceIdType.MESH
        )
    for d in range(1, clips):
        pl.semaphore_signal(
            barrier, inc=1, device_id={"clip": lax.rem(clip + d, clips)}, device_id_type=pl.DeviceIdType.MESH
        )
    pl.semaphore_wait(barrier, frames + clips - 2)

    def send_to(target, r, at, sems):
        @pl.when(target < me)
        def _():
            far_copy(0, me, r, at, tq_in, sems(0), target).start()
            far_copy(1, me, r, at, tc_in, sems(1), target).start()

        @pl.when(target > me)
        def _():
            far_copy(0, me, r, at, tk_in, sems(0), target).start()
            far_copy(1, me, r, at, tv_in, sems(1), target).start()

    def send_far(p):
        for d in others:
            send_to(chip_at(d) * 2 + core, piece_rows(p), p, lambda part: cross_send.at[part, d, p])

    for p in range(min(AHEAD, pieces)):
        send_far(p)
    for c in range(CHUNKS):
        send_to(mate, rows(c), c, lambda part: mate_send.at[part, c])

    raw_s[...] = jnp.zeros_like(raw_s)
    grad_s[...] = jnp.zeros_like(grad_s)
    logit_rows[...] = jnp.zeros_like(logit_rows)
    logit_heads[...] = jnp.zeros_like(logit_heads)
    for load in loads:
        load.wait()

    lane_row = lax.broadcasted_iota(jnp.int32, (1, LANES), 1)
    sharp_lanes = jnp.zeros((1, LANES), F32)
    for h in range(heads):
        sharp_lanes = jnp.where(lane_row == h, sharp[1, h], sharp_lanes)
    lane = lax.broadcasted_iota(jnp.int32, (block, LANES), 1)
    place = jnp.full((block, LANES), me, jnp.int32)

    def spatial(h):
        at = pl.ds(pl.multiple_of(h * width, width), width)
        query, key, value, cotangent = sq[:, at], sk[:, at], sv[:, at], sc[:, at]
        sharpness = sharp[0, h]
        raw = contract(query, key, 1, 1) * inv
        scores = raw * sharpness
        exponent = jnp.exp(scores - jnp.max(scores, axis=1, keepdims=True))
        weights = exponent * (1.0 / jnp.sum(exponent, axis=1, keepdims=True))
        weight_grad = contract(cotangent, value, 1, 1)
        delta = jnp.sum(weights * weight_grad, axis=1, keepdims=True)
        score_grad = weights * (weight_grad - delta)
        low = score_grad.astype(BF16)
        factor = sharpness * inv
        sdq[:, at] = (contract(low, key, 1, 0) * factor).astype(BF16)
        sdk[:, at] = (contract(low, query, 0, 0) * factor).astype(BF16)
        logit_heads[pl.ds(h, 1), :] = jnp.sum(score_grad * raw, axis=0, keepdims=True)

    def dots(left, right):
        out = jnp.zeros((block, LANES), F32)
        for h in range(heads):
            product = left(cols(h)).astype(F32) * right(cols(h)).astype(F32)
            out = jnp.where(lane == h, jnp.sum(product, axis=1, keepdims=True), out)
        return out

    def spread(mix, at):
        return jnp.broadcast_to(mix[:, at : at + 1], (block, width))

    def fold(low, high, body, start):
        if isinstance(low, int) and isinstance(high, int):
            for i in range(low, high):
                start = body(i, start)
            return start
        return lax.fori_loop(low, high, body, start)

    def store(which, c):
        src, dst = ((tdq, tdq_out), (tdk, tdk_out), (tdv, tdv_out))[which]
        return pltpu.make_async_copy(src.at[rows(c)], dst.at[rows(c)], store_sem.at[which, c])

    def row_part(c, own):
        r = rows(c)
        known = isinstance(own, int)
        for part in range(2):
            far_here(part, mate, r, c)
            for d in others:
                for p in range(SPLIT):
                    far_here(part, chip_at(d) * 2 + 1 - core, piece_rows(c * SPLIT + p), c * SPLIT + p)
        raw_own = dots(lambda s: tq[r, s], lambda s: tk[r, s]) * inv
        grad_own = dots(lambda s: tc[r, s], lambda s: tv[r, s])

        def pair(j):
            return (
                dots(lambda s: tq[r, s], lambda s: far[0, j, r, s]) * inv,
                dots(lambda s: tc[r, s], lambda s: far[1, j, r, s]),
            )

        if known:
            pairs = [pair(j) for j in range(own)]
        else:

            @pl.loop(0, own)
            def _(j):
                raw_s[j], grad_s[j] = pair(j)

            pairs = [(raw_s[j], grad_s[j]) for j in range(frames - 1)]

        def seen(j, x, other):
            return x if known else jnp.where(place > j, x, other)

        scores_own = raw_own * sharp_lanes
        scores = [x * sharp_lanes for x, _ in pairs]
        top = scores_own
        for j, x in enumerate(scores):
            top = jnp.maximum(top, seen(j, x, scores_own))
        exponent_own = jnp.exp(scores_own - top)
        exponent = [seen(j, jnp.exp(x - top), 0.0) for j, x in enumerate(scores)]
        total, mean = exponent_own, exponent_own * grad_own
        for e, (_, g) in zip(exponent, pairs):
            total, mean = total + e, mean + e * g
        over = 1.0 / total
        delta = mean * over

        def mixed(e, g):
            weights = e * over
            score_grad = weights * (g - delta)
            return score_grad, jnp.where(lane < HALF, weights, pltpu.roll(score_grad, HALF, 1)).astype(BF16)

        score_grad, mix_own = mixed(exponent_own, grad_own)
        mix_out[own, r] = mix_own
        share_sum = score_grad * raw_own

        for j, (raw, grad) in enumerate(pairs):
            score_grad, mix = mixed(exponent[j], grad)
            share_sum = share_sum + score_grad * raw

            def send_mix(j=j, mix=mix):
                mix_out[j, r] = mix
                remote(
                    mix_out.at[j, r], mix_in.at[me, r], mix_send.at[j, c], mix_recv.at[me, c], "frame", j
                ).start()

            if known:
                send_mix()
            else:
                pl.when(j < own)(send_mix)

        logit_rows[...] += share_sum

        for first in range(0, heads, HEADS_AT_ONCE):
            some = range(first, min(first + HEADS_AT_ONCE, heads))

            def add_key(j, sums):
                mix = mix_out[j, r].astype(F32)
                return tuple(
                    t + spread(mix, HALF + h) * far[0, j, r, cols(h)].astype(F32) for t, h in zip(sums, some)
                )

            mix = mix_own.astype(F32)
            sums = tuple(spread(mix, HALF + h) * tk[r, cols(h)].astype(F32) for h in some)
            sums = fold(0, own, add_key, sums)
            for t, h in zip(sums, some):
                tdq[r, cols(h)] = (t * (sharp[1, h] * inv)).astype(BF16)
        store(0, c).start()

    def column_part(c, own):
        r = rows(c)

        def arrived(i, carry):
            remote(
                mix_out.at[me, r], mix_in.at[i, r], mix_send.at[me, c], mix_recv.at[i, c], "frame", mate
            ).wait_recv()
            return carry

        fold(own + 1, frames, arrived, 0)

        for first in range(0, heads, HEADS_AT_ONCE):
            some = range(first, min(first + HEADS_AT_ONCE, heads))

            def add_row(i, sums):
                mix = mix_in[i, r].astype(F32)
                return tuple(
                    (
                        v + spread(mix, h) * far[1, i, r, cols(h)].astype(F32),
                        k + spread(mix, HALF + h) * far[0, i, r, cols(h)].astype(F32),
                    )
                    for (v, k), h in zip(sums, some)
                )

            mix = mix_out[own, r].astype(F32)
            sums = tuple(
                (
                    spread(mix, h) * tc[r, cols(h)].astype(F32),
                    spread(mix, HALF + h) * tq[r, cols(h)].astype(F32),
                )
                for h in some
            )
            sums = fold(own + 1, frames, add_row, sums)
            for (v, k), h in zip(sums, some):
                tdv[r, cols(h)] = v.astype(BF16)
                tdk[r, cols(h)] = (k * (sharp[1, h] * inv)).astype(BF16)
        store(1, c).start()
        store(2, c).start()

    def as_frame(work, c):
        if frames > WRITTEN_OUT:
            work(c, me)
            return
        for f in range(frames):
            pl.when(me == f)(functools.partial(work, c, f))

    def share(buffer, send, recv, axis, mine, size):
        for d in range(1, size):
            remote(
                buffer.at[mine], buffer.at[mine], send.at[d], recv.at[mine], axis, lax.rem(mine + d, size)
            ).start()

    def shared(buffer, send, recv, axis, mine, size):
        for d in range(1, size):
            slot = lax.rem(mine + d, size)
            remote(buffer.at[slot], buffer.at[slot], send.at[d], recv.at[slot], axis, slot).wait_recv()
        total = buffer[0]
        for i in range(1, size):
            total = total + buffer[i]
        return total

    def take(p):
        for part in range(2):
            for d in others:
                slot = chip_at(d) * 2 + core
                far_here(part, slot, piece_rows(p), p)
                far_copy(
                    part, slot, piece_rows(p), p, far.at[part, slot], pass_send.at[part, d, p], mate
                ).start()

        @pl.when(p + AHEAD < pieces)
        def _():
            send_far(p + AHEAD)

    per_step = -(-heads // CHUNKS)

    def spatial_stores():
        return [
            pltpu.make_async_copy(src, dst, spatial_sem.at[i])
            for i, (src, dst) in enumerate(((sdq, sdq_out), (sdk, sdk_out)))
        ]

    def sum_here():
        per_head = jnp.sum(logit_heads[...], axis=1, keepdims=True)
        tall = logit_heads.shape[0]
        own_lane = lax.broadcasted_iota(jnp.int32, (tall, LANES), 0) == lax.broadcasted_iota(
            jnp.int32, (tall, LANES), 1
        )
        spatial_sum = jnp.sum(jnp.where(own_lane, per_head, 0.0), axis=0, keepdims=True)
        temporal_sum = jnp.sum(logit_rows[...], axis=0, keepdims=True)
        which = lax.broadcasted_iota(jnp.int32, (8, LANES), 0)
        sum_frame[me] = jnp.where(which == 0, spatial_sum, jnp.where(which == 1, temporal_sum, 0.0))
        share(sum_frame, frame_send, frame_recv, "frame", me, frames)

    def sum_frames():
        sum_clip[clip] = shared(sum_frame, frame_send, frame_recv, "frame", me, frames)
        share(sum_clip, clip_send, clip_recv, "clip", clip, clips)

    @pl.loop(0, CHUNKS + 2)
    def _(c):
        @pl.when(c < CHUNKS)
        def _():
            for t in range(per_step):
                h = c * per_step + t
                if heads % CHUNKS == 0:
                    spatial(h)
                else:
                    pl.when(h < heads)(functools.partial(spatial, h))
            take(c * SPLIT)

        @pl.when(c == CHUNKS - 1)
        def _():
            for copy in spatial_stores():
                copy.start()

        @pl.when((c >= 1) & (c <= CHUNKS))
        def _():
            as_frame(row_part, c - 1)

        pl.when(c == CHUNKS)(sum_here)
        pl.when(c == CHUNKS + 1)(sum_frames)

        @pl.when(c >= 2)
        def _():
            as_frame(column_part, c - 2)

        @pl.when(c < CHUNKS)
        def _():
            for p in range(1, SPLIT):
                take(c * SPLIT + p)

    total = shared(sum_clip, clip_send, clip_recv, "clip", clip, clips)
    logit[...] = total[0:2, 0:heads] * scale_norm

    for copy in spatial_stores():
        copy.wait()
    for d in range(1, frames):
        remote(sum_frame.at[me], sum_frame.at[me], frame_send.at[d], frame_recv.at[me], "frame", mate).wait_send()
    for d in range(1, clips):
        remote(sum_clip.at[clip], sum_clip.at[clip], clip_send.at[d], clip_recv.at[clip], "frame", mate).wait_send()

    @pl.loop(0, CHUNKS)
    def _(c):
        for part in range(2):
            far_copy(part, me, rows(c), c, tq_in, mate_send.at[part, c], mate).wait_send()

        for which in range(3):
            store(which, c).wait()

        @pl.loop(0, me)
        def _(j):
            r = rows(c)
            remote(
                mix_out.at[j, r], mix_in.at[me, r], mix_send.at[j, c], mix_recv.at[me, c], "frame", mate
            ).wait_send()


    @pl.loop(0, pieces)
    def _(p):
        for part in range(2):
            for d in others:
                slot, r = chip_at(d) * 2 + core, piece_rows(p)
                far_copy(part, me, r, p, tq_in, cross_send.at[part, d, p], mate).wait_send()
                far_copy(part, slot, r, p, far.at[part, slot], pass_send.at[part, d, p], mate).wait_send()


def store_kernel(*refs):
    count = (len(refs) - 2) // 3
    stages, load_sem, save_sem = refs[2 * count : 3 * count], refs[-2], refs[-1]
    steps = []
    for i in range(count):
        src, dst, stage = refs[i], refs[count + i], stages[i]
        cuts = 2 if src.shape[0] % 32 == 0 else 1
        tall = src.shape[0] // cuts
        for part in range(cuts):
            r = pl.ds(part * tall, tall)
            steps.append(
                (
                    pltpu.make_async_copy(src.at[r], stage.at[r], load_sem.at[i, part]),
                    pltpu.make_async_copy(stage.at[r], dst.at[r], save_sem.at[i, part]),
                )
            )
    for load, _ in steps:
        load.start()
    for load, save in steps:
        load.wait()
        save.start()
    for _, save in steps:
        save.wait()


def on_device(sq, sk, sv, sc, tq, tk, tv, tc, sharpness):
    frames, clips = lax.axis_size("frame"), lax.axis_size("clip")
    heads = sharpness.shape[1]
    full = sq.shape
    patches, features = full[2], full[3]
    block = patches // CHUNKS
    chips = frames // 2
    flat = [x.reshape(patches, features) for x in (sq, sk, sv, sc, tq, tk, tv, tc)]
    plane = jax.ShapeDtypeStruct((patches, features), BF16)
    scale_norm = 1.0 / math.sqrt(clips * full[0] * frames * full[1] * patches)
    dma = pltpu.SemaphoreType.DMA
    out = pl.pallas_call(
        functools.partial(kernel, frames, clips, heads, scale_norm),
        out_shape=(plane,) * 5 + (jax.ShapeDtypeStruct((2, heads), F32),),
        in_specs=[pl.BlockSpec(memory_space=pltpu.HBM)] * 9,
        out_specs=(pl.BlockSpec(memory_space=pltpu.HBM),) * OUTPUTS + (pl.BlockSpec(memory_space=pltpu.VMEM),),
        scratch_shapes=[pltpu.SMEM((2, heads), F32)]
        + [pltpu.VMEM((patches, features), BF16)] * (8 + OUTPUTS)
        + [
            pltpu.VMEM((2, frames, patches, features), BF16),
            pltpu.VMEM((frames, block, LANES), F32),
            pltpu.VMEM((frames, block, LANES), F32),
            pltpu.VMEM((frames, patches, LANES), BF16),
            pltpu.VMEM((frames, patches, LANES), BF16),
            pltpu.VMEM((block, LANES), F32),
            pltpu.VMEM((-(-heads // 8) * 8, patches), F32),
            pltpu.VMEM((frames, 8, LANES), F32),
            pltpu.VMEM((clips, 8, LANES), F32),
            dma((9,)),
            dma((2,)),
            dma((3, CHUNKS)),
            dma((2, chips, CHUNKS * SPLIT)),
            dma((2, CHUNKS)),
            dma((2, chips, CHUNKS * SPLIT)),
            dma((frames, CHUNKS)),
            dma((frames,)),
            dma((clips,)),
            dma((2, frames, CHUNKS * SPLIT)),
            dma((frames, CHUNKS)),
            dma((frames,)),
            dma((clips,)),
        ],
        compiler_params=pltpu.CompilerParams(
            collective_id=0, has_side_effects=True, vmem_limit_bytes=GRANT
        ),
    )(sharpness, *flat)
    out = pl.pallas_call(
        store_kernel,
        out_shape=(plane,) * 5 + (jax.ShapeDtypeStruct((2, heads), F32),),
        in_specs=[pl.BlockSpec(memory_space=pltpu.HBM)] * 6,
        out_specs=(pl.BlockSpec(memory_space=pltpu.HBM),) * 6,
        scratch_shapes=[pltpu.VMEM((patches, features), BF16)] * OUTPUTS
        + [pltpu.VMEM((2, heads), F32), dma((6, 2)), dma((6, 2))],
        compiler_params=pltpu.CompilerParams(vmem_limit_bytes=GRANT),
    )(*out)
    return tuple(x.reshape(full) for x in out[:5]) + (out[5],)


def solution(mesh):
    part = P("clip", "frame", None, None)
    return jax.shard_map(
        on_device,
        mesh=mesh,
        in_specs=(part,) * 8 + (P(),),
        out_specs=(part,) * 5 + (P(),),
        check_vma=False,
    )
```

```python
import functools
import math

import jax
import jax.numpy as jnp
from jax import lax
from jax.experimental import pallas as pl
from jax.experimental.pallas import tpu as pltpu
from jax.sharding import PartitionSpec as P

F32 = jnp.float32
BF16 = jnp.bfloat16
LANES = 128
HALF = 64
CHUNKS = 8
SPLIT = 1
AHEAD = 2
SPATIAL_STEPS = 4
HEADS_AT_ONCE = 6
WRITTEN_OUT = 4
OUTPUTS = 5
GRANT = 61 * 1024 * 1024


def contract(left, right, left_dim, right_dim):
    return lax.dot_general(
        left, right, (((left_dim,), (right_dim,)), ((), ())), preferred_element_type=F32
    )


def kernel(
    frames,
    clips,
    heads,
    scale_norm,
    sharp_in,
    sq_in,
    sk_in,
    sv_in,
    sc_in,
    tq_in,
    tk_in,
    tv_in,
    tc_in,
    sdq_out,
    sdk_out,
    tdq_out,
    tdk_out,
    tdv_out,
    logit,
    sharp,
    sq,
    sk,
    sv,
    sc,
    tq,
    tk,
    tv,
    tc,
    sdq,
    sdk,
    tdq,
    tdk,
    tdv,
    far,
    raw_s,
    grad_s,
    mix_out,
    mix_in,
    logit_rows,
    logit_heads,
    sum_frame,
    sum_clip,
    load_sem,
    spatial_sem,
    store_sem,
    cross_send,
    mate_send,
    pass_send,
    mix_send,
    frame_send,
    clip_send,
    far_recv,
    mix_recv,
    frame_recv,
    clip_recv,
):
    me = lax.axis_index("frame")
    clip = lax.axis_index("clip")
    chips = frames // 2
    chip, core = me // 2, lax.rem(me, 2)
    mate = chip * 2 + 1 - core
    patches, features = sq.shape
    width = features // heads
    block = patches // CHUNKS
    pieces = CHUNKS * SPLIT
    piece = block // SPLIT
    inv = 1.0 / math.sqrt(width)
    others = range(1, chips)

    def rows(c):
        return pl.ds(pl.multiple_of(c * block, block), block)

    def cols(h):
        return slice(h * width, (h + 1) * width)

    def remote(src, dst, send, recv, axis, target):
        return pltpu.make_async_remote_copy(
            src_ref=src,
            dst_ref=dst,
            send_sem=send,
            recv_sem=recv,
            device_id={axis: target},
            device_id_type=pl.DeviceIdType.MESH,
        )

    def piece_rows(p):
        return pl.ds(pl.multiple_of(p * piece, piece), piece)

    def far_copy(part, slot, r, at, src, send, target):
        return remote(src.at[r], far.at[part, slot, r], send, far_recv.at[part, slot, at], "frame", target)

    def far_here(part, slot, r, at):
        far_copy(part, slot, r, at, far.at[part, slot], mate_send.at[part, 0], mate).wait_recv()

    def chip_at(d):
        return lax.rem(chip + d, chips)

    loads = [
        pltpu.make_async_copy(src, dst, load_sem.at[i])
        for i, (src, dst) in enumerate(
            ((sharp_in, sharp), (sq_in, sq), (sk_in, sk), (sv_in, sv), (sc_in, sc), (tq_in, tq), (tk_in, tk), (tv_in, tv), (tc_in, tc))
        )
    ]
    for load in loads:
        load.start()

    barrier = pltpu.get_barrier_semaphore()
    for d in range(1, frames):
        pl.semaphore_signal(
            barrier, inc=1, device_id={"frame": lax.rem(me + d, frames)}, device_id_type=pl.DeviceIdType.MESH
        )
    for d in range(1, clips):
        pl.semaphore_signal(
            barrier, inc=1, device_id={"clip": lax.rem(clip + d, clips)}, device_id_type=pl.DeviceIdType.MESH
        )
    pl.semaphore_wait(barrier, frames + clips - 2)

    def send_to(target, r, at, sems):
        @pl.when(target < me)
        def _():
            far_copy(0, me, r, at, tq_in, sems(0), target).start()
            far_copy(1, me, r, at, tc_in, sems(1), target).start()

        @pl.when(target > me)
        def _():
            far_copy(0, me, r, at, tk_in, sems(0), target).start()
            far_copy(1, me, r, at, tv_in, sems(1), target).start()

    def send_far(p):
        for d in others:
            send_to(chip_at(d) * 2 + core, piece_rows(p), p, lambda part: cross_send.at[part, d, p])

    for p in range(min(AHEAD, pieces)):
        send_far(p)
    for c in range(CHUNKS):
        send_to(mate, rows(c), c, lambda part: mate_send.at[part, c])

    raw_s[...] = jnp.zeros_like(raw_s)
    grad_s[...] = jnp.zeros_like(grad_s)
    logit_rows[...] = jnp.zeros_like(logit_rows)
    logit_heads[...] = jnp.zeros_like(logit_heads)
    for load in loads:
        load.wait()

    lane_row = lax.broadcasted_iota(jnp.int32, (1, LANES), 1)
    sharp_lanes = jnp.zeros((1, LANES), F32)
    for h in range(heads):
        sharp_lanes = jnp.where(lane_row == h, sharp[1, h], sharp_lanes)
    lane = lax.broadcasted_iota(jnp.int32, (block, LANES), 1)
    place = jnp.full((block, LANES), me, jnp.int32)

    def spatial(h):
        at = pl.ds(pl.multiple_of(h * width, width), width)
        query, key, value, cotangent = sq[:, at], sk[:, at], sv[:, at], sc[:, at]
        sharpness = sharp[0, h]
        raw = contract(query, key, 1, 1) * inv
        scores = raw * sharpness
        exponent = jnp.exp(scores - jnp.max(scores, axis=1, keepdims=True))
        weights = exponent * (1.0 / jnp.sum(exponent, axis=1, keepdims=True))
        weight_grad = contract(cotangent, value, 1, 1)
        delta = jnp.sum(weights * weight_grad, axis=1, keepdims=True)
        score_grad = weights * (weight_grad - delta)
        low = score_grad.astype(BF16)
        factor = sharpness * inv
        sdq[:, at] = (contract(low, key, 1, 0) * factor).astype(BF16)
        sdk[:, at] = (contract(low, query, 0, 0) * factor).astype(BF16)
        logit_heads[pl.ds(h, 1), :] = jnp.sum(score_grad * raw, axis=0, keepdims=True)

    def dots(left, right):
        out = jnp.zeros((block, LANES), F32)
        for h in range(heads):
            product = left(cols(h)).astype(F32) * right(cols(h)).astype(F32)
            out = jnp.where(lane == h, jnp.sum(product, axis=1, keepdims=True), out)
        return out

    def spread(mix, at):
        return jnp.broadcast_to(mix[:, at : at + 1], (block, width))

    def fold(low, high, body, start):
        if isinstance(low, int) and isinstance(high, int):
            for i in range(low, high):
                start = body(i, start)
            return start
        return lax.fori_loop(low, high, body, start)

    def store(which, c):
        src, dst = ((tdq, tdq_out), (tdk, tdk_out), (tdv, tdv_out))[which]
        return pltpu.make_async_copy(src.at[rows(c)], dst.at[rows(c)], store_sem.at[which, c])

    def row_part(c, own):
        r = rows(c)
        known = isinstance(own, int)
        for part in range(2):
            far_here(part, mate, r, c)
            for d in others:
                for p in range(SPLIT):
                    far_here(part, chip_at(d) * 2 + 1 - core, piece_rows(c * SPLIT + p), c * SPLIT + p)
        raw_own = dots(lambda s: tq[r, s], lambda s: tk[r, s]) * inv
        grad_own = dots(lambda s: tc[r, s], lambda s: tv[r, s])

        def pair(j):
            return (
                dots(lambda s: tq[r, s], lambda s: far[0, j, r, s]) * inv,
                dots(lambda s: tc[r, s], lambda s: far[1, j, r, s]),
            )

        if known:
            pairs = [pair(j) for j in range(own)]
        else:

            @pl.loop(0, own)
            def _(j):
                raw_s[j], grad_s[j] = pair(j)

            pairs = [(raw_s[j], grad_s[j]) for j in range(frames - 1)]

        def seen(j, x, other):
            return x if known else jnp.where(place > j, x, other)

        scores_own = raw_own * sharp_lanes
        scores = [x * sharp_lanes for x, _ in pairs]
        top = scores_own
        for j, x in enumerate(scores):
            top = jnp.maximum(top, seen(j, x, scores_own))
        exponent_own = jnp.exp(scores_own - top)
        exponent = [seen(j, jnp.exp(x - top), 0.0) for j, x in enumerate(scores)]
        total, mean = exponent_own, exponent_own * grad_own
        for e, (_, g) in zip(exponent, pairs):
            total, mean = total + e, mean + e * g
        over = 1.0 / total
        delta = mean * over

        def mixed(e, g):
            weights = e * over
            score_grad = weights * (g - delta)
            return score_grad, jnp.where(lane < HALF, weights, pltpu.roll(score_grad, HALF, 1)).astype(BF16)

        score_grad, mix_own = mixed(exponent_own, grad_own)
        mix_out[own, r] = mix_own
        share_sum = score_grad * raw_own

        for j, (raw, grad) in enumerate(pairs):
            score_grad, mix = mixed(exponent[j], grad)
            share_sum = share_sum + score_grad * raw

            def send_mix(j=j, mix=mix):
                mix_out[j, r] = mix
                remote(
                    mix_out.at[j, r], mix_in.at[me, r], mix_send.at[j, c], mix_recv.at[me, c], "frame", j
                ).start()

            if known:
                send_mix()
            else:
                pl.when(j < own)(send_mix)

        logit_rows[...] += share_sum

        for first in range(0, heads, HEADS_AT_ONCE):
            some = range(first, min(first + HEADS_AT_ONCE, heads))

            def add_key(j, sums):
                mix = mix_out[j, r].astype(F32)
                return tuple(
                    t + spread(mix, HALF + h) * far[0, j, r, cols(h)].astype(F32) for t, h in zip(sums, some)
                )

            mix = mix_own.astype(F32)
            sums = tuple(spread(mix, HALF + h) * tk[r, cols(h)].astype(F32) for h in some)
            sums = fold(0, own, add_key, sums)
            for t, h in zip(sums, some):
                tdq[r, cols(h)] = (t * (sharp[1, h] * inv)).astype(BF16)
        store(0, c).start()

    def column_part(c, own):
        r = rows(c)

        def arrived(i, carry):
            remote(
                mix_out.at[me, r], mix_in.at[i, r], mix_send.at[me, c], mix_recv.at[i, c], "frame", mate
            ).wait_recv()
            return carry

        fold(own + 1, frames, arrived, 0)

        for first in range(0, heads, HEADS_AT_ONCE):
            some = range(first, min(first + HEADS_AT_ONCE, heads))

            def add_row(i, sums):
                mix = mix_in[i, r].astype(F32)
                return tuple(
                    (
                        v + spread(mix, h) * far[1, i, r, cols(h)].astype(F32),
                        k + spread(mix, HALF + h) * far[0, i, r, cols(h)].astype(F32),
                    )
                    for (v, k), h in zip(sums, some)
                )

            mix = mix_out[own, r].astype(F32)
            sums = tuple(
                (
                    spread(mix, h) * tc[r, cols(h)].astype(F32),
                    spread(mix, HALF + h) * tq[r, cols(h)].astype(F32),
                )
                for h in some
            )
            sums = fold(own + 1, frames, add_row, sums)
            for (v, k), h in zip(sums, some):
                tdv[r, cols(h)] = v.astype(BF16)
                tdk[r, cols(h)] = (k * (sharp[1, h] * inv)).astype(BF16)
        store(1, c).start()
        store(2, c).start()

    def as_frame(work, c):
        if frames > WRITTEN_OUT:
            work(c, me)
            return
        for f in range(frames):
            pl.when(me == f)(functools.partial(work, c, f))

    def share(buffer, send, recv, axis, mine, size):
        for d in range(1, size):
            remote(
                buffer.at[mine], buffer.at[mine], send.at[d], recv.at[mine], axis, lax.rem(mine + d, size)
            ).start()

    def shared(buffer, send, recv, axis, mine, size):
        for d in range(1, size):
            slot = lax.rem(mine + d, size)
            remote(buffer.at[slot], buffer.at[slot], send.at[d], recv.at[slot], axis, slot).wait_recv()
        total = buffer[0]
        for i in range(1, size):
            total = total + buffer[i]
        return total

    def take(p):
        for part in range(2):
            for d in others:
                slot = chip_at(d) * 2 + core
                far_here(part, slot, piece_rows(p), p)
                far_copy(
                    part, slot, piece_rows(p), p, far.at[part, slot], pass_send.at[part, d, p], mate
                ).start()

        @pl.when(p + AHEAD < pieces)
        def _():
            send_far(p + AHEAD)

    per_step = -(-heads // SPATIAL_STEPS)

    def spatial_stores():
        return [
            pltpu.make_async_copy(src, dst, spatial_sem.at[i])
            for i, (src, dst) in enumerate(((sdq, sdq_out), (sdk, sdk_out)))
        ]

    def sum_here():
        per_head = jnp.sum(logit_heads[...], axis=1, keepdims=True)
        tall = logit_heads.shape[0]
        own_lane = lax.broadcasted_iota(jnp.int32, (tall, LANES), 0) == lax.broadcasted_iota(
            jnp.int32, (tall, LANES), 1
        )
        spatial_sum = jnp.sum(jnp.where(own_lane, per_head, 0.0), axis=0, keepdims=True)
        temporal_sum = jnp.sum(logit_rows[...], axis=0, keepdims=True)
        which = lax.broadcasted_iota(jnp.int32, (8, LANES), 0)
        sum_frame[me] = jnp.where(which == 0, spatial_sum, jnp.where(which == 1, temporal_sum, 0.0))
        share(sum_frame, frame_send, frame_recv, "frame", me, frames)

    def sum_frames():
        sum_clip[clip] = shared(sum_frame, frame_send, frame_recv, "frame", me, frames)
        share(sum_clip, clip_send, clip_recv, "clip", clip, clips)

    @pl.loop(0, CHUNKS + 2)
    def _(c):
        @pl.when(c < CHUNKS)
        def _():
            if heads % SPATIAL_STEPS == 0:

                @pl.when(c < SPATIAL_STEPS)
                def _():
                    for t in range(per_step):
                        spatial(c * per_step + t)

            else:
                for t in range(per_step):
                    h = c * per_step + t
                    pl.when(h < heads)(functools.partial(spatial, h))
            take(c * SPLIT)

        @pl.when(c == SPATIAL_STEPS)
        def _():
            for copy in spatial_stores():
                copy.start()

        @pl.when((c >= 1) & (c <= CHUNKS))
        def _():
            as_frame(row_part, c - 1)

        pl.when(c == CHUNKS)(sum_here)
        pl.when(c == CHUNKS + 1)(sum_frames)

        @pl.when(c >= 2)
        def _():
            as_frame(column_part, c - 2)

        @pl.when(c < CHUNKS)
        def _():
            for p in range(1, SPLIT):
                take(c * SPLIT + p)

    total = shared(sum_clip, clip_send, clip_recv, "clip", clip, clips)
    logit[...] = total[0:2, 0:heads] * scale_norm

    for copy in spatial_stores():
        copy.wait()
    for d in range(1, frames):
        remote(sum_frame.at[me], sum_frame.at[me], frame_send.at[d], frame_recv.at[me], "frame", mate).wait_send()
    for d in range(1, clips):
        remote(sum_clip.at[clip], sum_clip.at[clip], clip_send.at[d], clip_recv.at[clip], "frame", mate).wait_send()

    @pl.loop(0, CHUNKS)
    def _(c):
        for part in range(2):
            far_copy(part, me, rows(c), c, tq_in, mate_send.at[part, c], mate).wait_send()

        for which in range(3):
            store(which, c).wait()

        @pl.loop(0, me)
        def _(j):
            r = rows(c)
            remote(
                mix_out.at[j, r], mix_in.at[me, r], mix_send.at[j, c], mix_recv.at[me, c], "frame", mate
            ).wait_send()


    @pl.loop(0, pieces)
    def _(p):
        for part in range(2):
            for d in others:
                slot, r = chip_at(d) * 2 + core, piece_rows(p)
                far_copy(part, me, r, p, tq_in, cross_send.at[part, d, p], mate).wait_send()
                far_copy(part, slot, r, p, far.at[part, slot], pass_send.at[part, d, p], mate).wait_send()


def store_kernel(*refs):
    count = (len(refs) - 2) // 3
    stages, load_sem, save_sem = refs[2 * count : 3 * count], refs[-2], refs[-1]
    steps = []
    for i in range(count):
        src, dst, stage = refs[i], refs[count + i], stages[i]
        cuts = 2 if src.shape[0] % 32 == 0 else 1
        tall = src.shape[0] // cuts
        for part in range(cuts):
            r = pl.ds(part * tall, tall)
            steps.append(
                (
                    pltpu.make_async_copy(src.at[r], stage.at[r], load_sem.at[i, part]),
                    pltpu.make_async_copy(stage.at[r], dst.at[r], save_sem.at[i, part]),
                )
            )
    for load, _ in steps:
        load.start()
    for load, save in steps:
        load.wait()
        save.start()
    for _, save in steps:
        save.wait()


def on_device(sq, sk, sv, sc, tq, tk, tv, tc, sharpness):
    frames, clips = lax.axis_size("frame"), lax.axis_size("clip")
    heads = sharpness.shape[1]
    full = sq.shape
    patches, features = full[2], full[3]
    block = patches // CHUNKS
    chips = frames // 2
    flat = [x.reshape(patches, features) for x in (sq, sk, sv, sc, tq, tk, tv, tc)]
    plane = jax.ShapeDtypeStruct((patches, features), BF16)
    scale_norm = 1.0 / math.sqrt(clips * full[0] * frames * full[1] * patches)
    dma = pltpu.SemaphoreType.DMA
    out = pl.pallas_call(
        functools.partial(kernel, frames, clips, heads, scale_norm),
        out_shape=(plane,) * 5 + (jax.ShapeDtypeStruct((2, heads), F32),),
        in_specs=[pl.BlockSpec(memory_space=pltpu.HBM)] * 9,
        out_specs=(pl.BlockSpec(memory_space=pltpu.HBM),) * OUTPUTS + (pl.BlockSpec(memory_space=pltpu.VMEM),),
        scratch_shapes=[pltpu.SMEM((2, heads), F32)]
        + [pltpu.VMEM((patches, features), BF16)] * (8 + OUTPUTS)
        + [
            pltpu.VMEM((2, frames, patches, features), BF16),
            pltpu.VMEM((frames, block, LANES), F32),
            pltpu.VMEM((frames, block, LANES), F32),
            pltpu.VMEM((frames, patches, LANES), BF16),
            pltpu.VMEM((frames, patches, LANES), BF16),
            pltpu.VMEM((block, LANES), F32),
            pltpu.VMEM((-(-heads // 8) * 8, patches), F32),
            pltpu.VMEM((frames, 8, LANES), F32),
            pltpu.VMEM((clips, 8, LANES), F32),
            dma((9,)),
            dma((2,)),
            dma((3, CHUNKS)),
            dma((2, chips, CHUNKS * SPLIT)),
            dma((2, CHUNKS)),
            dma((2, chips, CHUNKS * SPLIT)),
            dma((frames, CHUNKS)),
            dma((frames,)),
            dma((clips,)),
            dma((2, frames, CHUNKS * SPLIT)),
            dma((frames, CHUNKS)),
            dma((frames,)),
            dma((clips,)),
        ],
        compiler_params=pltpu.CompilerParams(
            collective_id=0, has_side_effects=True, vmem_limit_bytes=GRANT
        ),
    )(sharpness, *flat)
    out = pl.pallas_call(
        store_kernel,
        out_shape=(plane,) * 5 + (jax.ShapeDtypeStruct((2, heads), F32),),
        in_specs=[pl.BlockSpec(memory_space=pltpu.HBM)] * 6,
        out_specs=(pl.BlockSpec(memory_space=pltpu.HBM),) * 6,
        scratch_shapes=[pltpu.VMEM((patches, features), BF16)] * OUTPUTS
        + [pltpu.VMEM((2, heads), F32), dma((6, 2)), dma((6, 2))],
        compiler_params=pltpu.CompilerParams(vmem_limit_bytes=GRANT),
    )(*out)
    return tuple(x.reshape(full) for x in out[:5]) + (out[5],)


def solution(mesh):
    part = P("clip", "frame", None, None)
    return jax.shard_map(
        on_device,
        mesh=mesh,
        in_specs=(part,) * 8 + (P(),),
        out_specs=(part,) * 5 + (P(),),
        check_vma=False,
    )
```

```python
import functools
import math

import jax
import jax.numpy as jnp
from jax import lax
from jax.experimental import pallas as pl
from jax.experimental.pallas import tpu as pltpu
from jax.sharding import PartitionSpec as P

F32 = jnp.float32
BF16 = jnp.bfloat16
LANES = 128
HALF = 64
CHUNKS = 4
SPLIT = 2
AHEAD = 3
SPATIAL_STEPS = 3
HEADS_AT_ONCE = 6
WRITTEN_OUT = 4
OUTPUTS = 5
GRANT = 61 * 1024 * 1024


def contract(left, right, left_dim, right_dim):
    return lax.dot_general(
        left, right, (((left_dim,), (right_dim,)), ((), ())), preferred_element_type=F32
    )


def kernel(
    frames,
    clips,
    heads,
    scale_norm,
    sharp_in,
    sq_in,
    sk_in,
    sv_in,
    sc_in,
    tq_in,
    tk_in,
    tv_in,
    tc_in,
    sdq_out,
    sdk_out,
    tdq_out,
    tdk_out,
    tdv_out,
    logit,
    sharp,
    sq,
    sk,
    sv,
    sc,
    tq,
    tk,
    tv,
    tc,
    sdq,
    sdk,
    tdq,
    tdk,
    tdv,
    far,
    raw_s,
    grad_s,
    mix_out,
    mix_in,
    logit_rows,
    logit_heads,
    sum_frame,
    sum_clip,
    load_sem,
    spatial_sem,
    store_sem,
    cross_send,
    mate_send,
    pass_send,
    mix_send,
    frame_send,
    clip_send,
    far_recv,
    mix_recv,
    frame_recv,
    clip_recv,
):
    me = lax.axis_index("frame")
    clip = lax.axis_index("clip")
    chips = frames // 2
    chip, core = me // 2, lax.rem(me, 2)
    mate = chip * 2 + 1 - core
    patches, features = sq.shape
    width = features // heads
    block = patches // CHUNKS
    pieces = CHUNKS * SPLIT
    piece = block // SPLIT
    inv = 1.0 / math.sqrt(width)
    others = range(1, chips)

    def rows(c):
        return pl.ds(pl.multiple_of(c * block, block), block)

    def cols(h):
        return slice(h * width, (h + 1) * width)

    def remote(src, dst, send, recv, axis, target):
        return pltpu.make_async_remote_copy(
            src_ref=src,
            dst_ref=dst,
            send_sem=send,
            recv_sem=recv,
            device_id={axis: target},
            device_id_type=pl.DeviceIdType.MESH,
        )

    def piece_rows(p):
        return pl.ds(pl.multiple_of(p * piece, piece), piece)

    def far_copy(part, slot, r, at, src, send, target):
        return remote(src.at[r], far.at[part, slot, r], send, far_recv.at[part, slot, at], "frame", target)

    def far_here(part, slot, r, at):
        far_copy(part, slot, r, at, far.at[part, slot], mate_send.at[part, 0], mate).wait_recv()

    def chip_at(d):
        return lax.rem(chip + d, chips)

    loads = [
        pltpu.make_async_copy(src, dst, load_sem.at[i])
        for i, (src, dst) in enumerate(
            ((sharp_in, sharp), (sq_in, sq), (sk_in, sk), (sv_in, sv), (sc_in, sc), (tq_in, tq), (tk_in, tk), (tv_in, tv), (tc_in, tc))
        )
    ]
    for load in loads:
        load.start()

    barrier = pltpu.get_barrier_semaphore()
    for d in range(1, frames):
        pl.semaphore_signal(
            barrier, inc=1, device_id={"frame": lax.rem(me + d, frames)}, device_id_type=pl.DeviceIdType.MESH
        )
    for d in range(1, clips):
        pl.semaphore_signal(
            barrier, inc=1, device_id={"clip": lax.rem(clip + d, clips)}, device_id_type=pl.DeviceIdType.MESH
        )
    pl.semaphore_wait(barrier, frames + clips - 2)

    def send_to(target, r, at, sems):
        @pl.when(target < me)
        def _():
            far_copy(0, me, r, at, tq_in, sems(0), target).start()
            far_copy(1, me, r, at, tc_in, sems(1), target).start()

        @pl.when(target > me)
        def _():
            far_copy(0, me, r, at, tk_in, sems(0), target).start()
            far_copy(1, me, r, at, tv_in, sems(1), target).start()

    def send_far(p):
        for d in others:
            send_to(chip_at(d) * 2 + core, piece_rows(p), p, lambda part: cross_send.at[part, d, p])

    for p in range(min(AHEAD, pieces)):
        send_far(p)
    for c in range(CHUNKS):
        send_to(mate, rows(c), c, lambda part: mate_send.at[part, c])

    raw_s[...] = jnp.zeros_like(raw_s)
    grad_s[...] = jnp.zeros_like(grad_s)
    logit_rows[...] = jnp.zeros_like(logit_rows)
    logit_heads[...] = jnp.zeros_like(logit_heads)
    for load in loads:
        load.wait()

    lane_row = lax.broadcasted_iota(jnp.int32, (1, LANES), 1)
    sharp_lanes = jnp.zeros((1, LANES), F32)
    for h in range(heads):
        sharp_lanes = jnp.where(lane_row == h, sharp[1, h], sharp_lanes)
    lane = lax.broadcasted_iota(jnp.int32, (block, LANES), 1)
    place = jnp.full((block, LANES), me, jnp.int32)

    def spatial(h):
        at = pl.ds(pl.multiple_of(h * width, width), width)
        query, key, value, cotangent = sq[:, at], sk[:, at], sv[:, at], sc[:, at]
        sharpness = sharp[0, h]
        raw = contract(query, key, 1, 1) * inv
        scores = raw * sharpness
        exponent = jnp.exp(scores - jnp.max(scores, axis=1, keepdims=True))
        weights = exponent * (1.0 / jnp.sum(exponent, axis=1, keepdims=True))
        weight_grad = contract(cotangent, value, 1, 1)
        delta = jnp.sum(weights * weight_grad, axis=1, keepdims=True)
        score_grad = weights * (weight_grad - delta)
        low = score_grad.astype(BF16)
        factor = sharpness * inv
        sdq[:, at] = (contract(low, key, 1, 0) * factor).astype(BF16)
        sdk[:, at] = (contract(low, query, 0, 0) * factor).astype(BF16)
        logit_heads[pl.ds(h, 1), :] = jnp.sum(score_grad * raw, axis=0, keepdims=True)

    def dots(left, right):
        out = jnp.zeros((block, LANES), F32)
        for h in range(heads):
            product = left(cols(h)).astype(F32) * right(cols(h)).astype(F32)
            out = jnp.where(lane == h, jnp.sum(product, axis=1, keepdims=True), out)
        return out

    def spread(mix, at):
        return jnp.broadcast_to(mix[:, at : at + 1], (block, width))

    def fold(low, high, body, start):
        if isinstance(low, int) and isinstance(high, int):
            for i in range(low, high):
                start = body(i, start)
            return start
        return lax.fori_loop(low, high, body, start)

    def store(which, c):
        src, dst = ((tdq, tdq_out), (tdk, tdk_out), (tdv, tdv_out))[which]
        return pltpu.make_async_copy(src.at[rows(c)], dst.at[rows(c)], store_sem.at[which, c])

    def row_part(c, own):
        r = rows(c)
        known = isinstance(own, int)
        for part in range(2):
            far_here(part, mate, r, c)
            for d in others:
                for p in range(SPLIT):
                    far_here(part, chip_at(d) * 2 + 1 - core, piece_rows(c * SPLIT + p), c * SPLIT + p)
        raw_own = dots(lambda s: tq[r, s], lambda s: tk[r, s]) * inv
        grad_own = dots(lambda s: tc[r, s], lambda s: tv[r, s])

        def pair(j):
            return (
                dots(lambda s: tq[r, s], lambda s: far[0, j, r, s]) * inv,
                dots(lambda s: tc[r, s], lambda s: far[1, j, r, s]),
            )

        if known:
            pairs = [pair(j) for j in range(own)]
        else:

            @pl.loop(0, own)
            def _(j):
                raw_s[j], grad_s[j] = pair(j)

            pairs = [(raw_s[j], grad_s[j]) for j in range(frames - 1)]

        def seen(j, x, other):
            return x if known else jnp.where(place > j, x, other)

        scores_own = raw_own * sharp_lanes
        scores = [x * sharp_lanes for x, _ in pairs]
        top = scores_own
        for j, x in enumerate(scores):
            top = jnp.maximum(top, seen(j, x, scores_own))
        exponent_own = jnp.exp(scores_own - top)
        exponent = [seen(j, jnp.exp(x - top), 0.0) for j, x in enumerate(scores)]
        total, mean = exponent_own, exponent_own * grad_own
        for e, (_, g) in zip(exponent, pairs):
            total, mean = total + e, mean + e * g
        over = 1.0 / total
        delta = mean * over

        def mixed(e, g):
            weights = e * over
            score_grad = weights * (g - delta)
            return score_grad, jnp.where(lane < HALF, weights, pltpu.roll(score_grad, HALF, 1)).astype(BF16)

        score_grad, mix_own = mixed(exponent_own, grad_own)
        mix_out[own, r] = mix_own
        share_sum = score_grad * raw_own

        for j, (raw, grad) in enumerate(pairs):
            score_grad, mix = mixed(exponent[j], grad)
            share_sum = share_sum + score_grad * raw

            def send_mix(j=j, mix=mix):
                mix_out[j, r] = mix
                remote(
                    mix_out.at[j, r], mix_in.at[me, r], mix_send.at[j, c], mix_recv.at[me, c], "frame", j
                ).start()

            if known:
                send_mix()
            else:
                pl.when(j < own)(send_mix)

        logit_rows[...] += share_sum

        for first in range(0, heads, HEADS_AT_ONCE):
            some = range(first, min(first + HEADS_AT_ONCE, heads))

            def add_key(j, sums):
                mix = mix_out[j, r].astype(F32)
                return tuple(
                    t + spread(mix, HALF + h) * far[0, j, r, cols(h)].astype(F32) for t, h in zip(sums, some)
                )

            mix = mix_own.astype(F32)
            sums = tuple(spread(mix, HALF + h) * tk[r, cols(h)].astype(F32) for h in some)
            sums = fold(0, own, add_key, sums)
            for t, h in zip(sums, some):
                tdq[r, cols(h)] = (t * (sharp[1, h] * inv)).astype(BF16)
        store(0, c).start()

    def column_part(c, own):
        r = rows(c)

        def arrived(i, carry):
            remote(
                mix_out.at[me, r], mix_in.at[i, r], mix_send.at[me, c], mix_recv.at[i, c], "frame", mate
            ).wait_recv()
            return carry

        fold(own + 1, frames, arrived, 0)

        for first in range(0, heads, HEADS_AT_ONCE):
            some = range(first, min(first + HEADS_AT_ONCE, heads))

            def add_row(i, sums):
                mix = mix_in[i, r].astype(F32)
                return tuple(
                    (
                        v + spread(mix, h) * far[1, i, r, cols(h)].astype(F32),
                        k + spread(mix, HALF + h) * far[0, i, r, cols(h)].astype(F32),
                    )
                    for (v, k), h in zip(sums, some)
                )

            mix = mix_out[own, r].astype(F32)
            sums = tuple(
                (
                    spread(mix, h) * tc[r, cols(h)].astype(F32),
                    spread(mix, HALF + h) * tq[r, cols(h)].astype(F32),
                )
                for h in some
            )
            sums = fold(own + 1, frames, add_row, sums)
            for (v, k), h in zip(sums, some):
                tdv[r, cols(h)] = v.astype(BF16)
                tdk[r, cols(h)] = (k * (sharp[1, h] * inv)).astype(BF16)
        store(1, c).start()
        store(2, c).start()

    def as_frame(work, c):
        if frames > WRITTEN_OUT:
            work(c, me)
            return
        for f in range(frames):
            pl.when(me == f)(functools.partial(work, c, f))

    def share(buffer, send, recv, axis, mine, size):
        for d in range(1, size):
            remote(
                buffer.at[mine], buffer.at[mine], send.at[d], recv.at[mine], axis, lax.rem(mine + d, size)
            ).start()

    def shared(buffer, send, recv, axis, mine, size):
        for d in range(1, size):
            slot = lax.rem(mine + d, size)
            remote(buffer.at[slot], buffer.at[slot], send.at[d], recv.at[slot], axis, slot).wait_recv()
        total = buffer[0]
        for i in range(1, size):
            total = total + buffer[i]
        return total

    def take(p):
        for part in range(2):
            for d in others:
                slot = chip_at(d) * 2 + core
                far_here(part, slot, piece_rows(p), p)
                far_copy(
                    part, slot, piece_rows(p), p, far.at[part, slot], pass_send.at[part, d, p], mate
                ).start()

        @pl.when(p + AHEAD < pieces)
        def _():
            send_far(p + AHEAD)

    per_step = -(-heads // SPATIAL_STEPS)

    def spatial_stores():
        return [
            pltpu.make_async_copy(src, dst, spatial_sem.at[i])
            for i, (src, dst) in enumerate(((sdq, sdq_out), (sdk, sdk_out)))
        ]

    def sum_here():
        per_head = jnp.sum(logit_heads[...], axis=1, keepdims=True)
        tall = logit_heads.shape[0]
        own_lane = lax.broadcasted_iota(jnp.int32, (tall, LANES), 0) == lax.broadcasted_iota(
            jnp.int32, (tall, LANES), 1
        )
        spatial_sum = jnp.sum(jnp.where(own_lane, per_head, 0.0), axis=0, keepdims=True)
        temporal_sum = jnp.sum(logit_rows[...], axis=0, keepdims=True)
        which = lax.broadcasted_iota(jnp.int32, (8, LANES), 0)
        sum_frame[me] = jnp.where(which == 0, spatial_sum, jnp.where(which == 1, temporal_sum, 0.0))
        share(sum_frame, frame_send, frame_recv, "frame", me, frames)

    def sum_frames():
        sum_clip[clip] = shared(sum_frame, frame_send, frame_recv, "frame", me, frames)
        share(sum_clip, clip_send, clip_recv, "clip", clip, clips)

    @pl.loop(0, CHUNKS + 2)
    def _(c):
        @pl.when(c < CHUNKS)
        def _():
            if heads % SPATIAL_STEPS == 0:

                @pl.when(c < SPATIAL_STEPS)
                def _():
                    for t in range(per_step):
                        spatial(c * per_step + t)

            else:
                for t in range(per_step):
                    h = c * per_step + t
                    pl.when(h < heads)(functools.partial(spatial, h))
            take(c * SPLIT)

        @pl.when(c == SPATIAL_STEPS)
        def _():
            for copy in spatial_stores():
                copy.start()

        @pl.when((c >= 1) & (c <= CHUNKS))
        def _():
            as_frame(row_part, c - 1)

        pl.when(c == CHUNKS)(sum_here)
        pl.when(c == CHUNKS + 1)(sum_frames)

        @pl.when(c >= 2)
        def _():
            as_frame(column_part, c - 2)

        @pl.when(c < CHUNKS)
        def _():
            for p in range(1, SPLIT):
                take(c * SPLIT + p)

    total = shared(sum_clip, clip_send, clip_recv, "clip", clip, clips)
    logit[...] = total[0:2, 0:heads] * scale_norm

    for copy in spatial_stores():
        copy.wait()
    for d in range(1, frames):
        remote(sum_frame.at[me], sum_frame.at[me], frame_send.at[d], frame_recv.at[me], "frame", mate).wait_send()
    for d in range(1, clips):
        remote(sum_clip.at[clip], sum_clip.at[clip], clip_send.at[d], clip_recv.at[clip], "frame", mate).wait_send()

    @pl.loop(0, CHUNKS)
    def _(c):
        for part in range(2):
            far_copy(part, me, rows(c), c, tq_in, mate_send.at[part, c], mate).wait_send()

        for which in range(3):
            store(which, c).wait()

        @pl.loop(0, me)
        def _(j):
            r = rows(c)
            remote(
                mix_out.at[j, r], mix_in.at[me, r], mix_send.at[j, c], mix_recv.at[me, c], "frame", mate
            ).wait_send()


    @pl.loop(0, pieces)
    def _(p):
        for part in range(2):
            for d in others:
                slot, r = chip_at(d) * 2 + core, piece_rows(p)
                far_copy(part, me, r, p, tq_in, cross_send.at[part, d, p], mate).wait_send()
                far_copy(part, slot, r, p, far.at[part, slot], pass_send.at[part, d, p], mate).wait_send()


def store_kernel(*refs):
    count = (len(refs) - 2) // 3
    stages, load_sem, save_sem = refs[2 * count : 3 * count], refs[-2], refs[-1]
    steps = []
    for i in range(count):
        src, dst, stage = refs[i], refs[count + i], stages[i]
        cuts = 2 if src.shape[0] % 32 == 0 else 1
        tall = src.shape[0] // cuts
        for part in range(cuts):
            r = pl.ds(part * tall, tall)
            steps.append(
                (
                    pltpu.make_async_copy(src.at[r], stage.at[r], load_sem.at[i, part]),
                    pltpu.make_async_copy(stage.at[r], dst.at[r], save_sem.at[i, part]),
                )
            )
    for load, _ in steps:
        load.start()
    for load, save in steps:
        load.wait()
        save.start()
    for _, save in steps:
        save.wait()


def on_device(sq, sk, sv, sc, tq, tk, tv, tc, sharpness):
    frames, clips = lax.axis_size("frame"), lax.axis_size("clip")
    heads = sharpness.shape[1]
    full = sq.shape
    patches, features = full[2], full[3]
    block = patches // CHUNKS
    chips = frames // 2
    flat = [x.reshape(patches, features) for x in (sq, sk, sv, sc, tq, tk, tv, tc)]
    plane = jax.ShapeDtypeStruct((patches, features), BF16)
    scale_norm = 1.0 / math.sqrt(clips * full[0] * frames * full[1] * patches)
    dma = pltpu.SemaphoreType.DMA
    out = pl.pallas_call(
        functools.partial(kernel, frames, clips, heads, scale_norm),
        out_shape=(plane,) * 5 + (jax.ShapeDtypeStruct((2, heads), F32),),
        in_specs=[pl.BlockSpec(memory_space=pltpu.HBM)] * 9,
        out_specs=(pl.BlockSpec(memory_space=pltpu.HBM),) * OUTPUTS + (pl.BlockSpec(memory_space=pltpu.VMEM),),
        scratch_shapes=[pltpu.SMEM((2, heads), F32)]
        + [pltpu.VMEM((patches, features), BF16)] * (8 + OUTPUTS)
        + [
            pltpu.VMEM((2, frames, patches, features), BF16),
            pltpu.VMEM((frames, block, LANES), F32),
            pltpu.VMEM((frames, block, LANES), F32),
            pltpu.VMEM((frames, patches, LANES), BF16),
            pltpu.VMEM((frames, patches, LANES), BF16),
            pltpu.VMEM((block, LANES), F32),
            pltpu.VMEM((-(-heads // 8) * 8, patches), F32),
            pltpu.VMEM((frames, 8, LANES), F32),
            pltpu.VMEM((clips, 8, LANES), F32),
            dma((9,)),
            dma((2,)),
            dma((3, CHUNKS)),
            dma((2, chips, CHUNKS * SPLIT)),
            dma((2, CHUNKS)),
            dma((2, chips, CHUNKS * SPLIT)),
            dma((frames, CHUNKS)),
            dma((frames,)),
            dma((clips,)),
            dma((2, frames, CHUNKS * SPLIT)),
            dma((frames, CHUNKS)),
            dma((frames,)),
            dma((clips,)),
        ],
        compiler_params=pltpu.CompilerParams(
            collective_id=0, has_side_effects=True, vmem_limit_bytes=GRANT
        ),
    )(sharpness, *flat)
    out = pl.pallas_call(
        store_kernel,
        out_shape=(plane,) * 5 + (jax.ShapeDtypeStruct((2, heads), F32),),
        in_specs=[pl.BlockSpec(memory_space=pltpu.HBM)] * 6,
        out_specs=(pl.BlockSpec(memory_space=pltpu.HBM),) * 6,
        scratch_shapes=[pltpu.VMEM((patches, features), BF16)] * OUTPUTS
        + [pltpu.VMEM((2, heads), F32), dma((6, 2)), dma((6, 2))],
        compiler_params=pltpu.CompilerParams(vmem_limit_bytes=GRANT),
    )(*out)
    return tuple(x.reshape(full) for x in out[:5]) + (out[5],)


def solution(mesh):
    part = P("clip", "frame", None, None)
    return jax.shard_map(
        on_device,
        mesh=mesh,
        in_specs=(part,) * 8 + (P(),),
        out_specs=(part,) * 5 + (P(),),
        check_vma=False,
    )
```
